32 devices in a mesh: own: 16 (over z, y, x), rep: 2 (over core).
Axes of the slice: x: 2, y: 2, z: 4, core: 2. Of those that a mesh axis runs over, the one named last changes fastest.
Arguments:
- sample_rows: bfloat16 [32768, 768], P(('own', 'rep'))
- destination: int32 [32768], P(('own', 'rep')), may hold values from 0 to 32767, as said below
- neighbours: int32 [32768, 4], P(('own', 'rep')), may hold values from 0 to 127, as said below
- centroids: bfloat16 [64, 2, 128, 768], P('own', 'rep'), may hold values from -6 to 6
Outputs:
- new_centroids: bfloat16 [64, 2, 128, 768], P('own', 'rep')
- row_cost: float32 [32768], P(('own', 'rep'))
The draws below stay inside these ranges and needn't reach their ends.
Inputs may be any that keep to these rules, and one draw needn't show every extreme that they name: destination is a permutation. Numbering devices own-major (device t = own index * 2 + rep index), ingested row i of device s goes to device t = destination[i] // 1024, and the rows that device t receives from device s fill its positions s * 32 up to (s + 1) * 32 - 1; every device sends exactly 32 rows to every device. `neighbours`: each regrouped row on the device with own index o and rep index r lists 4 different blocks a * 2 + r with a inside the grid and o * 4 - 1 <= a <= o * 4 + 4.
All inputs are finite; a program needn't handle non-finite values.
Results may differ from the reference program's by a relative error of at most 0.0075.
Values may be sent and summed in bfloat16 or wider, within the bound.
A program may use at most 64 MiB of HBM per device.

```python
import math
import jax
import jax.numpy as jnp
from jax import lax

D = 768
CB = 128
BLK = 4
NB = 4
ITERS = 2
ROWS = 1024
GA = 64
N_OWN = 16
N_REP = 2


def draw_sample_rows(key, part):
    total_rows = ROWS * N_OWN * N_REP
    return jax.random.normal(key, (total_rows, D), jnp.float32).astype(jnp.bfloat16)


def shuffle_rows(single_key):
    return jax.random.permutation(single_key, ROWS)


def draw_destination(key, part):
    sources = N_OWN * N_REP
    per_pair = ROWS // sources
    key_list = jax.random.split(key, sources)
    orders = jax.vmap(shuffle_rows)(key_list).astype(jnp.int32)
    source = jnp.arange(sources, dtype=jnp.int32)[:, None]
    target = orders // per_pair
    slot_index = orders % per_pair
    return (target * ROWS + source * per_pair + slot_index).reshape(sources * ROWS).astype(jnp.int32)


def draw_neighbours(key, part):
    total_rows = ROWS * N_OWN * N_REP
    window = BLK + 2
    position = jnp.arange(total_rows, dtype=jnp.int32)
    device = position // ROWS
    owner_index = device // N_REP
    column = device % N_REP
    first_block = owner_index * BLK - 1
    offsets = jnp.arange(window, dtype=jnp.int32)
    grid_first = first_block[:, None] + offsets[None, :]
    inside = (grid_first >= 0) & (grid_first < BLK * N_OWN)
    scores = jax.random.randint(key, (total_rows, window), 0, 1 << 20, dtype=jnp.int32) * 16 + offsets[None, :]
    scores = jnp.where(inside, scores, -1)
    picked = lax.top_k(scores, NB)[1]
    chosen = jnp.take_along_axis(grid_first, picked, axis=1)
    return (chosen * N_REP + column[:, None]).astype(jnp.int32)


def levels(stream_key, shape, pieces, least, high):
    factor_of = 1.0
    for dim, blocks in pieces:
        heights = jax.random.uniform(jax.random.fold_in(jax.random.fold_in(stream_key, 6), dim), (blocks,), jnp.float32, least / len(pieces), high / len(pieces))
        factor_of = factor_of * jnp.repeat(jnp.exp(heights), shape[dim] // blocks).reshape((-1,) + (1,) * (len(shape) - 1 - dim))
    return factor_of


def bell_draw(key, shape, scale, bound, pieces=(), held_as=jnp.bfloat16):
    values = scale * jax.random.normal(key, shape, jnp.float32)
    if pieces:
        values = values * levels(key, shape, pieces, -0.22, 0.18)
    return jnp.clip(values, -bound, bound).astype(held_as)


def setup_inputs(seed: int = 0) -> dict:
    splits = jax.random.split(jax.random.key(seed), 5)
    sample_rows = draw_sample_rows(jax.random.fold_in(splits[4], 71), 0)
    destination = draw_destination(jax.random.fold_in(splits[4], 71), 0)
    neighbours = draw_neighbours(jax.random.fold_in(splits[4], 71), 0)
    centroids = bell_draw(splits[3], (GA, N_REP, CB, D), 1.0, 6.0, ((0, 16), (1, 2)))
    return {"sample_rows": sample_rows, "destination": destination, "neighbours": neighbours, "centroids": centroids}


PRIOR = 1.0

def soft_assign(local_rows, local_ids, candidates):
    window, per_block, features = candidates.shape
    flat_blocks = candidates.reshape(window * per_block, features)
    inv_scale = 0.5 / math.sqrt(features)
    cross = lax.dot_general(local_rows, flat_blocks, (((1,), (1,)), ((), ())), preferred_element_type=jnp.float32)
    cand_wide = flat_blocks.astype(jnp.float32)
    cand_norm = lax.optimization_barrier(jnp.sum(cand_wide * cand_wide, axis=1))
    rows_wide = local_rows.astype(jnp.float32)
    rows_norm = lax.optimization_barrier(jnp.sum(rows_wide * rows_wide, axis=1))
    logits = (2.0 * cross - rows_norm[:, None] - cand_norm[None, :]) * inv_scale
    logits = logits.reshape(local_rows.shape[0], window, per_block)
    slots = jnp.arange(window, dtype=jnp.int32)
    chosen = jnp.any(local_ids[:, :, None] == slots[None, None, :], axis=1)[:, :, None]
    masked = jnp.where(chosen, logits, -jnp.inf)
    row_top = lax.optimization_barrier(jnp.max(masked, axis=(1, 2), keepdims=True))
    weights = jnp.where(chosen, jnp.exp(masked - row_top), 0.0)
    row_total = lax.optimization_barrier(jnp.sum(weights, axis=(1, 2), keepdims=True))
    responses = weights / row_total
    row_cost = -(row_top[:, 0, 0] + jnp.log(row_total[:, 0, 0]))
    resp_half = responses.reshape(local_rows.shape[0], window * per_block).astype(jnp.bfloat16)
    part_sums = lax.dot_general(resp_half, local_rows, (((0,), (0,)), ((), ())), preferred_element_type=jnp.float32)
    part_counts = lax.optimization_barrier(jnp.sum(responses, axis=0))
    return (part_sums.reshape(window, per_block, features), part_counts, row_cost)

def refresh(total, tally, previous):
    return ((total + PRIOR * previous.astype(jnp.float32)) / (tally[..., None] + PRIOR)).astype(jnp.bfloat16)

def reference(sample_rows, destination, neighbours, centroids):
    regrouped = jnp.zeros_like(sample_rows).at[destination].set(sample_rows)
    row_tiles = regrouped.reshape(N_OWN, N_REP, ROWS, D)
    owners = jnp.arange(N_OWN, dtype=jnp.int32)
    local_ids = (neighbours // N_REP).reshape(N_OWN, N_REP, ROWS, NB) - (owners * BLK - 1)[:, None, None, None]
    local_ids = local_ids.astype(jnp.int32)
    current = centroids.reshape(N_OWN, BLK, N_REP, CB, D)
    row_cost = jnp.zeros((N_OWN, N_REP, ROWS), jnp.float32)
    for iteration in range(ITERS):
        flat_grid = current.reshape(N_OWN * BLK, N_REP, CB, D)
        padded = jnp.pad(flat_grid, ((1, 1), (0, 0), (0, 0), (0, 0)))

        def one_owner(packed):
            tile_rows, tile_ids, owner_index = packed
            window = lax.dynamic_slice_in_dim(padded, owner_index * BLK, BLK + 2, 0)
            window = jnp.moveaxis(window, 1, 0)
            return jax.vmap(soft_assign)(tile_rows, tile_ids, window)
        part_sums, part_counts, row_cost = lax.map(one_owner, (row_tiles, local_ids, owners))
        zero_sums = jnp.zeros_like(part_sums[:1, :, 0])
        zero_counts = jnp.zeros_like(part_counts[:1, :, 0])
        from_left = jnp.concatenate([zero_sums, part_sums[:-1, :, BLK + 1]], axis=0)
        from_right = jnp.concatenate([part_sums[1:, :, 0], zero_sums], axis=0)
        total = part_sums[:, :, 1:BLK + 1].at[:, :, 0].add(from_left).at[:, :, BLK - 1].add(from_right)
        left_counts = jnp.concatenate([zero_counts, part_counts[:-1, :, BLK + 1]], axis=0)
        right_counts = jnp.concatenate([part_counts[1:, :, 0], zero_counts], axis=0)
        tally = part_counts[:, :, 1:BLK + 1].at[:, :, 0].add(left_counts).at[:, :, BLK - 1].add(right_counts)
        previous = jnp.moveaxis(current, 2, 1)
        fresh = refresh(total, tally, previous)
        current = jnp.moveaxis(fresh, 1, 2)
    return (current.reshape(N_OWN * BLK, N_REP, CB, D), row_cost.reshape(N_OWN * N_REP * ROWS))
```

```python
import functools
import math

import jax
import jax.numpy as jnp
from jax import lax
from jax.experimental import pallas as pl
from jax.experimental.pallas import tpu as pltpu
from jax.sharding import PartitionSpec as P

ITERS = 2
PRIOR = 1.0
MESH = pl.DeviceIdType.MESH
F32 = jnp.float32
BF16 = jnp.bfloat16
LN2 = math.log(2.0)
NT = (((1,), (1,)), ((), ()))
NN = (((1,), (0,)), ((), ()))


def dot(a, b, dims):
    return lax.dot_general(a, b, dims, preferred_element_type=F32)


def kernel(
    fused, own_n, rep_n, pp, chunk, order, *refs
):
    (nbr_ref, dest_ref, rows_ref, cent_ref, out_ref, cost_ref,
     arr, outb, cand, cn, bias, xn, acc, macc, lg, resp, snd, rcv, msnd, mrcv,
     a_send, a_recv, c_send, c_recv, s_send, s_recv, m_send, m_recv) = refs
    count, feat = rows_ref.shape
    slots = nbr_ref.shape[0]
    cb = rcv.shape[2]
    blk = cent_ref.shape[0] // cb
    win = blk + 2
    wc = win * cb
    nchunk = count // chunk
    total_n = own_n * rep_n
    own = lax.axis_index("own")
    rep = lax.axis_index("rep")
    me = own * rep_n + rep
    sides = (own > 0, own < own_n - 1)
    scale2 = 0.5 / math.sqrt(feat) / LN2

    barrier = pltpu.get_barrier_semaphore()
    if fused:
        def greet(k, carry):
            t = lax.rem(me + k, total_n)
            pl.semaphore_signal(
                barrier, inc=1, device_id=(lax.div(t, rep_n), lax.rem(t, rep_n)), device_id_type=MESH
            )
            return carry

        lax.fori_loop(1, total_n, greet, 0)
    else:
        for d in range(2):
            @pl.when(sides[d])
            def _():
                pl.semaphore_signal(
                    barrier, inc=1, device_id=(own + 2 * d - 1, rep), device_id_type=MESH
                )

    zero_block = jnp.zeros((cb, feat), BF16)
    for d in range(2):
        @pl.when(jnp.logical_not(sides[1 - d]))
        def _():
            place = 0 if d else win - 1
            cand[place * cb : (place + 1) * cb, :] = zero_block
            for q in range(3):
                rcv[d, q] = zero_block
                mrcv[d, q] = jnp.zeros((8, 128), F32)
    cand[cb : (blk + 1) * cb, :] = cent_ref[...]

    def block_copy(d):
        src = 0 if d == 0 else (blk - 1) * cb
        dst = (win - 1) * cb if d == 0 else 0
        return pltpu.make_async_remote_copy(
            src_ref=cent_ref.at[pl.ds(src, cb)],
            dst_ref=cand.at[pl.ds(dst, cb)],
            send_sem=c_send.at[d],
            recv_sem=c_recv.at[d],
            device_id=(own + 2 * d - 1, rep),
            device_id_type=MESH,
        )

    def edge_copies(d, q):
        where = (own + 2 * d - 1, rep)
        return [
            pltpu.make_async_remote_copy(
                src_ref=a.at[d, q], dst_ref=b.at[d, q], send_sem=s.at[d, q], recv_sem=r.at[d, q],
                device_id=where, device_id_type=MESH,
            )
            for a, b, s, r in ((msnd, mrcv, m_send, m_recv), (snd, rcv, s_send, s_recv))
        ]

    def row_copy(src, t):
        return pltpu.make_async_remote_copy(
            src_ref=outb.at[pl.ds(pl.multiple_of(t * pp, pp), pp)],
            dst_ref=arr.at[pl.ds(pl.multiple_of(src * pp, pp), pp)],
            send_sem=a_send.at[t],
            recv_sem=a_recv.at[src],
            device_id=(lax.div(t, rep_n), lax.rem(t, rep_n)),
            device_id_type=MESH,
        )

    per = chunk // pp if fused else 1
    group = lax.div(me, per) if fused else 0

    def pack(g):
        base = pl.multiple_of(g * chunk, chunk)
        pos = lax.broadcasted_iota(jnp.int32, (chunk, count), 0)
        bits = pp.bit_length() - 1
        want = lax.shift_right_logical(pos, bits) * count + (pos & (pp - 1))
        hot = dest_ref[...] - (g * per * count + me * pp)
        pick = jnp.where(want == hot, 1.0, 0.0).astype(BF16)
        outb[pl.ds(base, chunk), :] = dot(pick, rows_ref[...], NN).astype(BF16)

    def wait_entry():
        if fused:
            pl.semaphore_wait(barrier, total_n - 1)
        else:
            for d in range(2):
                @pl.when(sides[d])
                def _():
                    pl.semaphore_wait(barrier, 1)
        for d in range(2):
            @pl.when(sides[d])
            def _():
                block_copy(d).start()

    def send_group(g):
        def send(k, carry):
            t = g * per + lax.rem(me + k, per)

            @pl.when(t != me)
            def _():
                row_copy(me, t).start()

            return carry

        lax.fori_loop(0, per, send, 0)

    if fused:
        for n, j in enumerate(order):
            g = lax.rem(group + j, nchunk)
            pack(g)
            if n == 0:
                wait_entry()
            send_group(g)
        mine = pl.ds(pl.multiple_of(me * pp, pp), pp)
        arr[mine, :] = outb[mine, :]
        rows = arr
    else:
        wait_entry()
        rows = rows_ref

    for c in range(nchunk):
        ids = nbr_ref[:, c * chunk : (c + 1) * chunk]
        for w in range(win):
            block = (own * blk - 1 + w) * rep_n + rep
            hit = ids[0:1] == block
            for m in range(1, slots):
                hit = jnp.logical_or(hit, ids[m : m + 1] == block)
            bias[c, w : w + 1, :] = jnp.where(hit, 0.0, -jnp.inf)

    acc[...] = jnp.zeros_like(acc)
    macc[...] = jnp.zeros_like(macc)

    def norms(low, high):
        wide = cand[low:high, :].astype(F32)
        cn[low:high, :] = jnp.sum(wide * wide, axis=1, keepdims=True) * scale2

    norms(cb, (blk + 1) * cb)
    for d in range(2):
        @pl.when(sides[1 - d])
        def _():
            block_copy(d).wait_recv()
    norms(0, cb)
    norms(wc - cb, wc)

    def respond(c):
        raw = [lg[c, w * cb : (w + 1) * cb, :] + bias[c, w : w + 1, :] for w in range(win)]
        top = functools.reduce(jnp.maximum, raw)
        top = jnp.max(top, axis=0, keepdims=True)
        raw = [jnp.exp2(r - top) for r in raw]
        whole = jnp.sum(functools.reduce(jnp.add, raw), axis=0, keepdims=True)
        inverse = 1.0 / whole
        for w in range(win):
            part = slice(w * cb, (w + 1) * cb)
            got = raw[w] * inverse
            resp[c, part, :] = got.astype(BF16)
            folded = got[:, 0:128]
            for i in range(1, chunk // 128):
                folded = folded + got[:, i * 128 : (i + 1) * 128]
            macc[part, :] += folded
        return top, whole

    def chunk_rows(c):
        return rows[pl.ds(pl.multiple_of(c * chunk, chunk), chunk), :]

    def arrive(c):
        if fused:
            def wait(k, carry):
                s = c * per + k

                @pl.when(s != me)
                def _():
                    row_copy(s, s).wait_recv()

                return carry

            lax.fori_loop(0, per, wait, 0)
        x = chunk_rows(c)
        lg[c] = dot(cand[...], x, NT) * (2.0 * scale2) - cn[...]
        respond(c)
        wide = x.astype(F32)
        wide = wide * wide
        high = wide.astype(BF16)
        low = (wide - high.astype(F32)).astype(BF16)
        ones = jnp.ones((8, feat), BF16)
        xn[c] = dot(ones, high, NT) + dot(ones, low, NT)

    def early(j, carry):
        c = lax.rem(group + j, nchunk)
        arrive(c)
        acc[...] += dot(resp[c], chunk_rows(c), NN)
        return carry

    if nchunk > 1:
        lax.fori_loop(0, nchunk - 1, early, 0)
    last = lax.rem(group + nchunk - 1, nchunk)
    arrive(last)

    def part_of(w):
        return slice(w * cb, (w + 1) * cb)

    def mass_of(w):
        return jnp.sum(macc[part_of(w), :], axis=1, keepdims=True)

    def ship(d, q, w):
        snd[d, q] = acc[part_of(w), :].astype(BF16)
        wide = jnp.transpose(jnp.broadcast_to(mass_of(w), (cb, 128)))
        msnd[d, q] = wide[0:8, :]

        @pl.when(sides[d])
        def _():
            for copy in edge_copies(d, q):
                copy.start()

    def land(d, q):
        @pl.when(sides[1 - d])
        def _():
            for copy in edge_copies(d, q):
                copy.wait_recv()

    def fresh(w, source=None):
        total = acc[part_of(w), :] + cand[part_of(w), :].astype(F32)
        tally = mass_of(w) + PRIOR
        if source is not None:
            total = total + rcv[source].astype(F32)
            arrived = jnp.transpose(jnp.broadcast_to(mrcv[source][0:1, :], (128, 128)))
            tally = tally + arrived[:, 0:1]
        return (total * (1.0 / tally)).astype(BF16)

    def finish(w):
        acc[part_of(w), :] += dot(resp[last, part_of(w), :], chunk_rows(last), NN)

    def score(w):
        norms(w * cb, (w + 1) * cb)
        for c in range(nchunk):
            lg[c, part_of(w), :] = (
                dot(cand[part_of(w), :], chunk_rows(c), NT) * (2.0 * scale2) - cn[part_of(w), :]
            )

    for d, q, w in ((0, 0, 0), (1, 0, win - 1), (0, 1, 1), (1, 1, win - 2)):
        finish(w)
        ship(d, q, w)
    for w in range(2, win - 2):
        finish(w)
    for w in range(2, win - 2):
        cand[part_of(w), :] = fresh(w)
        score(w)
    for d, q, w in ((1, 0, 1), (0, 0, win - 2), (1, 1, 0), (0, 1, win - 1)):
        land(d, q)
        cand[part_of(w), :] = fresh(w, (d, q))
        score(w)

    macc[...] = jnp.zeros_like(macc)

    def second(c, carry):
        top, whole = respond(c)
        cost_ref[pl.ds(c, 1), :] = xn[c][0:1, :] * (scale2 * LN2) - (top * LN2 + jnp.log(whole))
        return carry

    lax.fori_loop(0, nchunk, second, 0)

    def gather(w):
        sums = dot(resp[0, part_of(w), :], chunk_rows(0), NN)
        for c in range(1, nchunk):
            sums = sums + dot(resp[c, part_of(w), :], chunk_rows(c), NN)
        acc[part_of(w), :] = sums

    for d, w in ((0, 0), (1, win - 1)):
        gather(w)
        ship(d, 2, w)
    for w in range(1, win - 1):
        gather(w)
    for w in range(2, win - 2):
        out_ref[part_of(w - 1), :] = fresh(w)
    for d, w in ((1, 1), (0, win - 2)):
        land(d, 2)
        out_ref[part_of(w - 1), :] = fresh(w, (d, 2))

    for d in range(2):
        @pl.when(sides[d])
        def _():
            block_copy(d).wait_send()
            for q in range(3):
                for copy in edge_copies(d, q):
                    copy.wait_send()

    if fused:
        def drain(k, carry):
            row_copy(me, lax.rem(me + k, total_n)).wait_send()
            return carry

        lax.fori_loop(1, total_n, drain, 0)


def regroup(sample_rows, destination, own_n, rep_n):
    count, feat = sample_rows.shape
    pp = count // (own_n * rep_n)
    target = destination // count
    outgoing = jnp.zeros((own_n, rep_n, pp, feat), sample_rows.dtype)
    outgoing = outgoing.at[target // rep_n, target % rep_n, destination % pp].set(sample_rows)
    arrived = lax.all_to_all(
        lax.all_to_all(outgoing, "own", split_axis=0, concat_axis=0, tiled=True),
        "rep", split_axis=1, concat_axis=1, tiled=True,
    )
    return arrived.reshape(count, feat)


def per_device(sample_rows, destination, neighbours, centroids):
    own_n = lax.axis_size("own")
    rep_n = lax.axis_size("rep")
    count, feat = sample_rows.shape
    blk, _, cb, _ = centroids.shape
    pp = count // (own_n * rep_n)
    chunk = min(256, count)
    nchunk = count // chunk
    fused = pp % 16 == 0 and pp & (pp - 1) == 0 and chunk % pp == 0
    rows = sample_rows if fused else regroup(sample_rows, destination, own_n, rep_n)
    order = [j for j in (2, 1, 3) if j < nchunk] + list(range(4, nchunk)) + [0]
    wc = (blk + 2) * cb
    total_n = own_n * rep_n
    dma = pltpu.SemaphoreType.DMA
    vmem = pl.BlockSpec(memory_space=pltpu.VMEM)
    staged = count if fused else 16
    out, cost = pl.pallas_call(
        functools.partial(kernel, fused, own_n, rep_n, pp, chunk, order),
        out_shape=(
            jax.ShapeDtypeStruct((blk * cb, feat), BF16),
            jax.ShapeDtypeStruct((nchunk, chunk), F32),
        ),
        in_specs=[vmem] * 4,
        out_specs=(vmem, vmem),
        scratch_shapes=[
            pltpu.VMEM((staged, feat), BF16),
            pltpu.VMEM((staged, feat), BF16),
            pltpu.VMEM((wc, feat), BF16),
            pltpu.VMEM((wc, 1), F32),
            pltpu.VMEM((nchunk, 8, chunk), F32),
            pltpu.VMEM((nchunk, 8, chunk), F32),
            pltpu.VMEM((wc, feat), F32),
            pltpu.VMEM((wc, 128), F32),
            pltpu.VMEM((nchunk, wc, chunk), F32),
            pltpu.VMEM((nchunk, wc, chunk), BF16),
            pltpu.VMEM((2, 3, cb, feat), BF16),
            pltpu.VMEM((2, 3, cb, feat), BF16),
            pltpu.VMEM((2, 3, 8, 128), F32),
            pltpu.VMEM((2, 3, 8, 128), F32),
            dma((total_n,)),
            dma((total_n,)),
            dma((2,)),
            dma((2,)),
            dma((2, 3)),
            dma((2, 3)),
            dma((2, 3)),
            dma((2, 3)),
        ],
        compiler_params=pltpu.CompilerParams(
            collective_id=0, has_side_effects=True, vmem_limit_bytes=48 * 1024 * 1024
        ),
    )(neighbours.T, destination.reshape(1, count), rows, centroids.reshape(blk * cb, feat))
    return out.reshape(centroids.shape), cost.reshape(count)


def solution(mesh):
    return jax.shard_map(
        per_device,
        mesh=mesh,
        in_specs=(
            P(("own", "rep"), None),
            P(("own", "rep")),
            P(("own", "rep"), None),
            P("own", "rep", None, None),
        ),
        out_specs=(P("own", "rep", None, None), P(("own", "rep"))),
        check_vma=False,
    )
```

```python
import functools
import math

import jax
import jax.numpy as jnp
from jax import lax
from jax.experimental import pallas as pl
from jax.experimental.pallas import tpu as pltpu
from jax.sharding import PartitionSpec as P

ITERS = 2
PRIOR = 1.0
MESH = pl.DeviceIdType.MESH
F32 = jnp.float32
BF16 = jnp.bfloat16
LN2 = math.log(2.0)
NT = (((1,), (1,)), ((), ()))
NN = (((1,), (0,)), ((), ()))


def dot(a, b, dims):
    return lax.dot_general(a, b, dims, preferred_element_type=F32)


def kernel(
    fused, own_n, rep_n, pp, chunk, order, *refs
):
    (nbr_in, dest_in, rows_in, cent_in, out_ref, cost_ref,
     nbr_ref, dest_ref, rows_ref, arr, outb, stat, cand, cn, bias, xn, acc, macc, lg, resp, snd, rcv, msnd, mrcv,
     a_send, a_recv, c_send, c_recv, s_send, s_recv, m_send, m_recv, load) = refs
    count, feat = rows_in.shape
    slots = nbr_ref.shape[0]
    cb = rcv.shape[2]
    blk = cent_in.shape[0] // cb
    win = blk + 2
    wc = win * cb
    nchunk = count // chunk
    total_n = own_n * rep_n
    own = lax.axis_index("own")
    rep = lax.axis_index("rep")
    me = own * rep_n + rep
    sides = (own > 0, own < own_n - 1)
    scale2 = 0.5 / math.sqrt(feat) / LN2

    loads = [
        pltpu.make_async_copy(a, b, load.at[i])
        for i, (a, b) in enumerate((
            (dest_in, dest_ref),
            (rows_in, rows_ref if fused else arr),
            (cent_in, cand.at[pl.ds(cb, blk * cb)]),
            (nbr_in, nbr_ref),
        ))
    ]
    for one in loads:
        one.start()
    barrier = pltpu.get_barrier_semaphore()
    if fused:
        def greet(k, carry):
            t = lax.rem(me + k, total_n)
            pl.semaphore_signal(
                barrier, inc=1, device_id=(lax.div(t, rep_n), lax.rem(t, rep_n)), device_id_type=MESH
            )
            return carry

        lax.fori_loop(1, total_n, greet, 0)
    else:
        for d in range(2):
            @pl.when(sides[d])
            def _():
                pl.semaphore_signal(
                    barrier, inc=1, device_id=(own + 2 * d - 1, rep), device_id_type=MESH
                )

    zero_block = jnp.zeros((cb, feat), BF16)
    for d in range(2):
        @pl.when(jnp.logical_not(sides[1 - d]))
        def _():
            place = 0 if d else win - 1
            cand[place * cb : (place + 1) * cb, :] = zero_block
            for q in range(3):
                rcv[d, q] = zero_block
                mrcv[d, q] = jnp.zeros((8, 128), F32)

    def block_copy(d):
        src = 0 if d == 0 else (blk - 1) * cb
        dst = (win - 1) * cb if d == 0 else 0
        return pltpu.make_async_remote_copy(
            src_ref=cent_in.at[pl.ds(src, cb)],
            dst_ref=cand.at[pl.ds(dst, cb)],
            send_sem=c_send.at[d],
            recv_sem=c_recv.at[d],
            device_id=(own + 2 * d - 1, rep),
            device_id_type=MESH,
        )

    def edge_copies(d, q):
        where = (own + 2 * d - 1, rep)
        return [
            pltpu.make_async_remote_copy(
                src_ref=a.at[d, q], dst_ref=b.at[d, q], send_sem=s.at[d, q], recv_sem=r.at[d, q],
                device_id=where, device_id_type=MESH,
            )
            for a, b, s, r in ((msnd, mrcv, m_send, m_recv), (snd, rcv, s_send, s_recv))
        ]

    def row_copy(src, t):
        return pltpu.make_async_remote_copy(
            src_ref=outb.at[pl.ds(pl.multiple_of(t * pp, pp), pp)],
            dst_ref=arr.at[pl.ds(pl.multiple_of(src * pp, pp), pp)],
            send_sem=a_send.at[t],
            recv_sem=a_recv.at[src],
            device_id=(lax.div(t, rep_n), lax.rem(t, rep_n)),
            device_id_type=MESH,
        )

    per = chunk // pp if fused else 1
    group = lax.div(me, per) if fused else 0

    def pack(g):
        base = pl.multiple_of(g * chunk, chunk)
        pos = lax.broadcasted_iota(jnp.int32, (chunk, count), 0)
        bits = pp.bit_length() - 1
        want = lax.shift_right_logical(pos, bits) * count + (pos & (pp - 1))
        hot = dest_ref[...] - (g * per * count + me * pp)
        pick = jnp.where(want == hot, 1.0, 0.0).astype(BF16)
        outb[pl.ds(base, chunk), :] = dot(pick, rows_ref[...], NN).astype(BF16)

    def wait_entry():
        if fused:
            pl.semaphore_wait(barrier, total_n - 1)
        else:
            for d in range(2):
                @pl.when(sides[d])
                def _():
                    pl.semaphore_wait(barrier, 1)
        for d in range(2):
            @pl.when(sides[d])
            def _():
                block_copy(d).start()

    def send_group(g):
        def send(k, carry):
            t = g * per + lax.rem(me + k, per)

            @pl.when(t != me)
            def _():
                row_copy(me, t).start()

            return carry

        lax.fori_loop(0, per, send, 0)

    loads[0].wait()
    loads[1].wait()
    if fused:
        for n, j in enumerate(order):
            g = lax.rem(group + j, nchunk)
            pack(g)
            if n == 0:
                wait_entry()
            send_group(g)
        mine = pl.ds(pl.multiple_of(me * pp, pp), pp)
        arr[mine, :] = outb[mine, :]
    else:
        wait_entry()
    rows = arr
    loads[2].wait()
    loads[3].wait()

    for c in range(nchunk):
        ids = nbr_ref[:, c * chunk : (c + 1) * chunk]
        for w in range(win):
            block = (own * blk - 1 + w) * rep_n + rep
            hit = ids[0:1] == block
            for m in range(1, slots):
                hit = jnp.logical_or(hit, ids[m : m + 1] == block)
            bias[c, w : w + 1, :] = jnp.where(hit, 0.0, -jnp.inf)

    acc[...] = jnp.zeros_like(acc)
    macc[...] = jnp.zeros_like(macc)

    def norms(low, high):
        wide = cand[low:high, :].astype(F32)
        cn[low:high, :] = jnp.sum(wide * wide, axis=1, keepdims=True) * scale2

    norms(cb, (blk + 1) * cb)
    for d in range(2):
        @pl.when(sides[1 - d])
        def _():
            block_copy(d).wait_recv()
    norms(0, cb)
    norms(wc - cb, wc)

    def fold(got):
        folded = got[:, 0:128]
        for i in range(1, chunk // 128):
            folded = folded + got[:, i * 128 : (i + 1) * 128]
        return folded

    def respond(c):
        raw = [lg[c, w * cb : (w + 1) * cb, :] + bias[c, w : w + 1, :] for w in range(win)]
        top = functools.reduce(jnp.maximum, raw)
        top = jnp.max(top, axis=0, keepdims=True)
        raw = [jnp.exp2(r - top) for r in raw]
        whole = jnp.sum(functools.reduce(jnp.add, raw), axis=0, keepdims=True)
        inverse = 1.0 / whole
        for w in range(win):
            part = slice(w * cb, (w + 1) * cb)
            got = raw[w] * inverse
            resp[c, part, :] = got.astype(BF16)
            macc[part, :] += fold(got)

    def chunk_rows(c):
        return rows[pl.ds(pl.multiple_of(c * chunk, chunk), chunk), :]

    def arrive(c):
        if fused:
            def wait(k, carry):
                s = c * per + k

                @pl.when(s != me)
                def _():
                    row_copy(s, s).wait_recv()

                return carry

            lax.fori_loop(0, per, wait, 0)
        x = chunk_rows(c)
        lg[c] = dot(cand[...], x, NT) * (2.0 * scale2) - cn[...]
        respond(c)
        wide = x.astype(F32)
        wide = wide * wide
        high = wide.astype(BF16)
        low = (wide - high.astype(F32)).astype(BF16)
        ones = jnp.ones((8, feat), BF16)
        xn[c] = dot(ones, high, NT) + dot(ones, low, NT)

    def early(j, carry):
        c = lax.rem(group + j, nchunk)
        arrive(c)
        acc[...] += dot(resp[c], chunk_rows(c), NN)
        return carry

    if nchunk > 1:
        lax.fori_loop(0, nchunk - 1, early, 0)
    last = lax.rem(group + nchunk - 1, nchunk)
    arrive(last)

    def part_of(w):
        return slice(w * cb, (w + 1) * cb)

    def mass_of(w):
        return jnp.sum(macc[part_of(w), :], axis=1, keepdims=True)

    def ship(d, q, w):
        snd[d, q] = acc[part_of(w), :].astype(BF16)
        wide = jnp.transpose(jnp.broadcast_to(mass_of(w), (cb, 128)))
        msnd[d, q] = wide[0:8, :]

        @pl.when(sides[d])
        def _():
            for copy in edge_copies(d, q):
                copy.start()

    def land(d, q):
        @pl.when(sides[1 - d])
        def _():
            for copy in edge_copies(d, q):
                copy.wait_recv()

    def fresh(w, source=None):
        total = acc[part_of(w), :] + cand[part_of(w), :].astype(F32)
        tally = mass_of(w) + PRIOR
        if source is not None:
            total = total + rcv[source].astype(F32)
            arrived = jnp.transpose(jnp.broadcast_to(mrcv[source][0:1, :], (128, 128)))
            tally = tally + arrived[:, 0:1]
        return (total * (1.0 / tally)).astype(BF16)

    def finish(w):
        acc[part_of(w), :] += dot(resp[last, part_of(w), :], chunk_rows(last), NN)

    def score(w):
        norms(w * cb, (w + 1) * cb)
        for c in range(nchunk):
            lg[c, part_of(w), :] = (
                dot(cand[part_of(w), :], chunk_rows(c), NT) * (2.0 * scale2) - cn[part_of(w), :]
            )

    for d, q, w in ((0, 0, 0), (1, 0, win - 1), (0, 1, 1), (1, 1, win - 2)):
        finish(w)
        ship(d, q, w)
    for w in range(2, win - 2):
        finish(w)
    for w in range(2, win - 2):
        cand[part_of(w), :] = fresh(w)
        score(w)
    def update(d, q, w):
        land(d, q)
        cand[part_of(w), :] = fresh(w, (d, q))
        score(w)

    update(1, 0, 1)
    update(0, 0, win - 2)

    def inner(c, carry):
        raw = [lg[c, part_of(w), :] + bias[c, w : w + 1, :] for w in range(1, win - 1)]
        top = jnp.max(functools.reduce(jnp.maximum, raw), axis=0, keepdims=True)
        raw = [jnp.exp2(r - top) for r in raw]
        for w in range(1, win - 1):
            lg[c, part_of(w), :] = raw[w - 1]
        stat[c, 0:1, :] = top
        stat[c, 1:2, :] = jnp.sum(functools.reduce(jnp.add, raw), axis=0, keepdims=True)
        return carry

    lax.fori_loop(0, nchunk, inner, 0)
    update(1, 1, 0)
    update(0, 1, win - 1)
    macc[...] = jnp.zeros_like(macc)

    def second(c, carry):
        ends = (0, win - 1)
        raw = [lg[c, part_of(w), :] + bias[c, w : w + 1, :] for w in ends]
        held = stat[c, 0:1, :]
        top = jnp.maximum(jnp.max(jnp.maximum(*raw), axis=0, keepdims=True), held)
        raw = [jnp.exp2(r - top) for r in raw]
        factor = jnp.exp2(held - top)
        whole = stat[c, 1:2, :] * factor + jnp.sum(raw[0] + raw[1], axis=0, keepdims=True)
        inverse = 1.0 / whole
        factor = factor * inverse
        for w in range(win):
            got = raw[ends.index(w)] * inverse if w in ends else lg[c, part_of(w), :] * factor
            resp[c, part_of(w), :] = got.astype(BF16)
            macc[part_of(w), :] += fold(got)
        cost_ref[pl.ds(c, 1), :] = xn[c][0:1, :] * (scale2 * LN2) - (top * LN2 + jnp.log(whole))
        return carry

    lax.fori_loop(0, nchunk, second, 0)

    def gather(w):
        sums = dot(resp[0, part_of(w), :], chunk_rows(0), NN)
        for c in range(1, nchunk):
            sums = sums + dot(resp[c, part_of(w), :], chunk_rows(c), NN)
        acc[part_of(w), :] = sums

    for d, w in ((0, 0), (1, win - 1)):
        gather(w)
        ship(d, 2, w)
    for w in range(1, win - 1):
        gather(w)
    for w in range(2, win - 2):
        out_ref[part_of(w - 1), :] = fresh(w)
    for d, w in ((1, 1), (0, win - 2)):
        land(d, 2)
        out_ref[part_of(w - 1), :] = fresh(w, (d, 2))

    for d in range(2):
        @pl.when(sides[d])
        def _():
            block_copy(d).wait_send()
            for q in range(3):
                for copy in edge_copies(d, q):
                    copy.wait_send()

    if fused:
        def drain(k, carry):
            row_copy(me, lax.rem(me + k, total_n)).wait_send()
            return carry

        lax.fori_loop(1, total_n, drain, 0)


def regroup(sample_rows, destination, own_n, rep_n):
    count, feat = sample_rows.shape
    pp = count // (own_n * rep_n)
    target = destination // count
    outgoing = jnp.zeros((own_n, rep_n, pp, feat), sample_rows.dtype)
    outgoing = outgoing.at[target // rep_n, target % rep_n, destination % pp].set(sample_rows)
    arrived = lax.all_to_all(
        lax.all_to_all(outgoing, "own", split_axis=0, concat_axis=0, tiled=True),
        "rep", split_axis=1, concat_axis=1, tiled=True,
    )
    return arrived.reshape(count, feat)


def per_device(sample_rows, destination, neighbours, centroids):
    own_n = lax.axis_size("own")
    rep_n = lax.axis_size("rep")
    count, feat = sample_rows.shape
    blk, _, cb, _ = centroids.shape
    pp = count // (own_n * rep_n)
    chunk = min(256, count)
    nchunk = count // chunk
    fused = pp % 16 == 0 and pp & (pp - 1) == 0 and chunk % pp == 0
    rows = sample_rows if fused else regroup(sample_rows, destination, own_n, rep_n)
    order = [j for j in (2, 1, 3) if j < nchunk] + list(range(4, nchunk)) + [0]
    wc = (blk + 2) * cb
    total_n = own_n * rep_n
    dma = pltpu.SemaphoreType.DMA
    vmem = pl.BlockSpec(memory_space=pltpu.VMEM)
    staged = count if fused else 16
    out, cost = pl.pallas_call(
        functools.partial(kernel, fused, own_n, rep_n, pp, chunk, order),
        out_shape=(
            jax.ShapeDtypeStruct((blk * cb, feat), BF16),
            jax.ShapeDtypeStruct((nchunk, chunk), F32),
        ),
        in_specs=[pl.BlockSpec(memory_space=pl.ANY)] * 4,
        out_specs=(vmem, vmem),
        scratch_shapes=[
            pltpu.VMEM((neighbours.shape[1], count), jnp.int32),
            pltpu.VMEM((1, count), jnp.int32),
            pltpu.VMEM((staged, feat), BF16),
            pltpu.VMEM((count, feat), BF16),
            pltpu.VMEM((staged, feat), BF16),
            pltpu.VMEM((nchunk, 8, chunk), F32),
            pltpu.VMEM((wc, feat), BF16),
            pltpu.VMEM((wc, 1), F32),
            pltpu.VMEM((nchunk, 8, chunk), F32),
            pltpu.VMEM((nchunk, 8, chunk), F32),
            pltpu.VMEM((wc, feat), F32),
            pltpu.VMEM((wc, 128), F32),
            pltpu.VMEM((nchunk, wc, chunk), F32),
            pltpu.VMEM((nchunk, wc, chunk), BF16),
            pltpu.VMEM((2, 3, cb, feat), BF16),
            pltpu.VMEM((2, 3, cb, feat), BF16),
            pltpu.VMEM((2, 3, 8, 128), F32),
            pltpu.VMEM((2, 3, 8, 128), F32),
            dma((total_n,)),
            dma((total_n,)),
            dma((2,)),
            dma((2,)),
            dma((2, 3)),
            dma((2, 3)),
            dma((2, 3)),
            dma((2, 3)),
            dma((4,)),
        ],
        compiler_params=pltpu.CompilerParams(
            collective_id=0, has_side_effects=True, vmem_limit_bytes=48 * 1024 * 1024
        ),
    )(neighbours.T, destination.reshape(1, count), rows, centroids.reshape(blk * cb, feat))
    return out.reshape(centroids.shape), cost.reshape(count)


def solution(mesh):
    return jax.shard_map(
        per_device,
        mesh=mesh,
        in_specs=(
            P(("own", "rep"), None),
            P(("own", "rep")),
            P(("own", "rep"), None),
            P("own", "rep", None, None),
        ),
        out_specs=(P("own", "rep", None, None), P(("own", "rep"))),
        check_vma=False,
    )
```

```python
import functools
import math

import jax
import jax.numpy as jnp
from jax import lax
from jax.experimental import pallas as pl
from jax.experimental.pallas import tpu as pltpu
from jax.sharding import PartitionSpec as P

ITERS = 2
PRIOR = 1.0
MESH = pl.DeviceIdType.MESH
F32 = jnp.float32
BF16 = jnp.bfloat16
LN2 = math.log(2.0)
NT = (((1,), (1,)), ((), ()))
NN = (((1,), (0,)), ((), ()))


def dot(a, b, dims):
    return lax.dot_general(a, b, dims, preferred_element_type=F32)


def kernel(
    fused, own_n, rep_n, pp, chunk, order, *refs
):
    (nbr_in, dest_in, rows_in, cent_in, out_ref, cost_ref,
     nbr_ref, dest_ref, rows_ref, arr, outb, stat, cand, cn, bias, xn, acc, macc, lg, resp, snd, rcv, msnd, mrcv,
     a_send, a_recv, c_send, c_recv, s_send, s_recv, m_send, m_recv, load,
     t_send, t_recv, f_send, f_recv, res, res_cost) = refs
    count, feat = rows_in.shape
    slots = nbr_ref.shape[0]
    cb = rcv.shape[2]
    blk = cent_in.shape[0] // cb
    win = blk + 2
    wc = win * cb
    nchunk = count // chunk
    lanes = chunk // 128
    total_n = own_n * rep_n
    own = lax.axis_index("own")
    rep = lax.axis_index("rep")
    me = own * rep_n + rep
    paired = fused and rep_n == 2 and own_n % 2 == 0

    def place_of(a, b):
        if not paired:
            return (a, b)
        odd = lax.rem(a, 2)
        return (a - odd + b, odd)

    work, col = place_of(own, rep)
    wid = work * rep_n + col
    moved = jnp.logical_and(paired, wid != me)
    stays = jnp.logical_not(moved)
    holds = (own > 0, own < own_n - 1)
    sides = (work > 0, work < own_n - 1)
    scale2 = 0.5 / math.sqrt(feat) / LN2

    loads = [
        pltpu.make_async_copy(a, b, load.at[i])
        for i, (a, b) in enumerate((
            (dest_in, dest_ref),
            (rows_in, rows_ref if fused else arr),
            (cent_in, cand.at[pl.ds(cb, blk * cb)]),
            (nbr_in, nbr_ref),
        ))
    ]
    def on(which, fn):
        if paired or which is stays:
            pl.when(which)(fn)

    def traded(src, dst, i, send=t_send, recv=t_recv):
        return pltpu.make_async_remote_copy(
            src_ref=src, dst_ref=dst, send_sem=send.at[i], recv_sem=recv.at[i],
            device_id=(work, col), device_id_type=MESH,
        )

    def trades():
        return [
            traded(nbr_in, nbr_ref, 0),
            traded(cent_in, cand.at[pl.ds(cb, blk * cb)], 1),
        ]

    def each(ops, act):
        def run():
            for one in ops():
                act(one)
        return run

    for one in loads[:2]:
        one.start()
    on(stays, each(lambda: loads[2:], lambda one: one.start()))
    barrier = pltpu.get_barrier_semaphore()
    if fused:
        def greet(k, carry):
            t = lax.rem(me + k, total_n)
            pl.semaphore_signal(
                barrier, inc=1, device_id=(lax.div(t, rep_n), lax.rem(t, rep_n)), device_id_type=MESH
            )
            return carry

        lax.fori_loop(1, total_n, greet, 0)
    else:
        for d in range(2):
            @pl.when(sides[d])
            def _():
                pl.semaphore_signal(
                    barrier, inc=1, device_id=(own + 2 * d - 1, rep), device_id_type=MESH
                )

    zero_block = jnp.zeros((cb, feat), BF16)
    for d in range(2):
        @pl.when(jnp.logical_not(sides[1 - d]))
        def _():
            place = 0 if d else win - 1
            cand[place * cb : (place + 1) * cb, :] = zero_block
            for q in range(3):
                rcv[d, q] = zero_block
                mrcv[d, q] = jnp.zeros((8, 128), F32)

    def block_copy(d):
        src = 0 if d == 0 else (blk - 1) * cb
        dst = (win - 1) * cb if d == 0 else 0
        return pltpu.make_async_remote_copy(
            src_ref=cent_in.at[pl.ds(src, cb)],
            dst_ref=cand.at[pl.ds(dst, cb)],
            send_sem=c_send.at[d],
            recv_sem=c_recv.at[d],
            device_id=place_of(own + 2 * d - 1, rep),
            device_id_type=MESH,
        )

    def edge_copies(d, q):
        where = place_of(work + 2 * d - 1, col)
        return [
            pltpu.make_async_remote_copy(
                src_ref=a.at[d, q], dst_ref=b.at[d, q], send_sem=s.at[d, q], recv_sem=r.at[d, q],
                device_id=where, device_id_type=MESH,
            )
            for a, b, s, r in ((msnd, mrcv, m_send, m_recv), (snd, rcv, s_send, s_recv))
        ]

    def row_copy(src, t):
        return pltpu.make_async_remote_copy(
            src_ref=outb.at[pl.ds(pl.multiple_of(t * pp, pp), pp)],
            dst_ref=arr.at[pl.ds(pl.multiple_of(src * pp, pp), pp)],
            send_sem=a_send.at[t],
            recv_sem=a_recv.at[src],
            device_id=place_of(lax.div(t, rep_n), lax.rem(t, rep_n)),
            device_id_type=MESH,
        )

    per = chunk // pp if fused else 1
    group = lax.div(me, per) if fused else 0

    def pack(g):
        base = pl.multiple_of(g * chunk, chunk)
        pos = lax.broadcasted_iota(jnp.int32, (chunk, count), 0)
        bits = pp.bit_length() - 1
        want = lax.shift_right_logical(pos, bits) * count + (pos & (pp - 1))
        hot = dest_ref[...] - (g * per * count + me * pp)
        pick = jnp.where(want == hot, 1.0, 0.0).astype(BF16)
        outb[pl.ds(base, chunk), :] = dot(pick, rows_ref[...], NN).astype(BF16)

    def wait_entry():
        if fused:
            pl.semaphore_wait(barrier, total_n - 1)
        else:
            for d in range(2):
                @pl.when(sides[d])
                def _():
                    pl.semaphore_wait(barrier, 1)
        on(moved, each(trades, lambda one: one.start()))
        for d in range(2):
            @pl.when(holds[d])
            def _():
                block_copy(d).start()

    def send_group(g):
        def send(k, carry):
            t = g * per + lax.rem(me + k, per)

            @pl.when(t != wid)
            def _():
                row_copy(me, t).start()

            return carry

        lax.fori_loop(0, per, send, 0)

    loads[0].wait()
    loads[1].wait()
    if fused:
        for n, j in enumerate(order):
            g = lax.rem(group + j, nchunk)
            pack(g)
            if n == 0:
                wait_entry()
            send_group(g)
        mine = pl.ds(pl.multiple_of(me * pp, pp), pp)
        kept = pl.ds(pl.multiple_of(wid * pp, pp), pp)
        arr[mine, :] = outb[kept, :]
    else:
        wait_entry()
    rows = arr
    on(stays, each(lambda: loads[2:], lambda one: one.wait()))
    on(moved, each(trades, lambda one: one.wait_recv()))

    for c in range(nchunk):
        ids = nbr_ref[:, c * chunk : (c + 1) * chunk]
        for w in range(win):
            block = (work * blk - 1 + w) * rep_n + col
            hit = ids[0:1] == block
            for m in range(1, slots):
                hit = jnp.logical_or(hit, ids[m : m + 1] == block)
            bias[c, w : w + 1, :] = jnp.where(hit, 0.0, -jnp.inf)

    acc[...] = jnp.zeros_like(acc)
    macc[...] = jnp.zeros_like(macc)

    def norms(low, high):
        wide = cand[low:high, :].astype(F32)
        cn[low:high, :] = jnp.sum(wide * wide, axis=1, keepdims=True) * scale2

    norms(cb, (blk + 1) * cb)
    for d in range(2):
        @pl.when(sides[1 - d])
        def _():
            block_copy(d).wait_recv()
    norms(0, cb)
    norms(wc - cb, wc)

    def fold(got):
        folded = got[:, 0:128]
        for i in range(1, chunk // 128):
            folded = folded + got[:, i * 128 : (i + 1) * 128]
        return folded

    def respond(c):
        raw = [lg[c, w * cb : (w + 1) * cb, :] + bias[c, w : w + 1, :] for w in range(win)]
        top = functools.reduce(jnp.maximum, raw)
        top = jnp.max(top, axis=0, keepdims=True)
        raw = [jnp.exp2(r - top) for r in raw]
        whole = jnp.sum(functools.reduce(jnp.add, raw), axis=0, keepdims=True)
        inverse = 1.0 / whole
        for w in range(win):
            part = slice(w * cb, (w + 1) * cb)
            got = raw[w] * inverse
            resp[c, part, :] = got.astype(BF16)
            macc[part, :] += fold(got)

    def chunk_rows(c):
        return rows[pl.ds(pl.multiple_of(c * chunk, chunk), chunk), :]

    def arrive(c):
        if fused:
            def wait(k, carry):
                s = c * per + k

                @pl.when(s != me)
                def _():
                    row_copy(s, s).wait_recv()

                return carry

            lax.fori_loop(0, per, wait, 0)
        x = chunk_rows(c)
        lg[c] = dot(cand[...], x, NT) * (2.0 * scale2) - cn[...]
        respond(c)
        wide = x.astype(F32)
        wide = wide * wide
        high = wide.astype(BF16)
        low = (wide - high.astype(F32)).astype(BF16)
        ones = jnp.ones((8, feat), BF16)
        xn[c] = dot(ones, high, NT) + dot(ones, low, NT)

    def early(j, carry):
        c = lax.rem(group + j, nchunk)
        arrive(c)
        acc[...] += dot(resp[c], chunk_rows(c), NN)
        return carry

    if nchunk > 1:
        lax.fori_loop(0, nchunk - 1, early, 0)
    last = lax.rem(group + nchunk - 1, nchunk)
    arrive(last)

    def part_of(w):
        return slice(w * cb, (w + 1) * cb)

    def mass_of(w):
        return jnp.sum(macc[part_of(w), :], axis=1, keepdims=True)

    def ship(d, q, w):
        snd[d, q] = acc[part_of(w), :].astype(BF16)
        wide = jnp.transpose(jnp.broadcast_to(mass_of(w), (cb, 128)))
        msnd[d, q] = wide[0:8, :]

        @pl.when(sides[d])
        def _():
            for copy in edge_copies(d, q):
                copy.start()

    def land(d, q):
        @pl.when(sides[1 - d])
        def _():
            for copy in edge_copies(d, q):
                copy.wait_recv()

    def fresh(w, source=None):
        total = acc[part_of(w), :] + cand[part_of(w), :].astype(F32)
        tally = mass_of(w) + PRIOR
        if source is not None:
            total = total + rcv[source].astype(F32)
            arrived = jnp.transpose(jnp.broadcast_to(mrcv[source][0:1, :], (128, 128)))
            tally = tally + arrived[:, 0:1]
        return (total * (1.0 / tally)).astype(BF16)

    def finish(w):
        acc[part_of(w), :] += dot(resp[last, part_of(w), :], chunk_rows(last), NN)

    def score(w):
        norms(w * cb, (w + 1) * cb)
        for c in range(nchunk):
            lg[c, part_of(w), :] = (
                dot(cand[part_of(w), :], chunk_rows(c), NT) * (2.0 * scale2) - cn[part_of(w), :]
            )

    for d, q, w in ((0, 0, 0), (1, 0, win - 1), (0, 1, 1), (1, 1, win - 2)):
        finish(w)
        ship(d, q, w)
    for w in range(2, win - 2):
        finish(w)
    for w in range(2, win - 2):
        cand[part_of(w), :] = fresh(w)
        score(w)
    def update(d, q, w):
        land(d, q)
        cand[part_of(w), :] = fresh(w, (d, q))
        score(w)

    update(1, 0, 1)
    update(0, 0, win - 2)

    def inner(c, carry):
        raw = [lg[c, part_of(w), :] + bias[c, w : w + 1, :] for w in range(1, win - 1)]
        top = jnp.max(functools.reduce(jnp.maximum, raw), axis=0, keepdims=True)
        raw = [jnp.exp2(r - top) for r in raw]
        for w in range(1, win - 1):
            lg[c, part_of(w), :] = raw[w - 1]
        stat[c, 0:1, :] = top
        stat[c, 1:2, :] = jnp.sum(functools.reduce(jnp.add, raw), axis=0, keepdims=True)
        return carry

    lax.fori_loop(0, nchunk, inner, 0)
    update(1, 1, 0)
    update(0, 1, win - 1)
    macc[...] = jnp.zeros_like(macc)

    def second(c, carry):
        ends = (0, win - 1)
        raw = [lg[c, part_of(w), :] + bias[c, w : w + 1, :] for w in ends]
        held = stat[c, 0:1, :]
        top = jnp.maximum(jnp.max(jnp.maximum(*raw), axis=0, keepdims=True), held)
        raw = [jnp.exp2(r - top) for r in raw]
        factor = jnp.exp2(held - top)
        whole = stat[c, 1:2, :] * factor + jnp.sum(raw[0] + raw[1], axis=0, keepdims=True)
        inverse = 1.0 / whole
        factor = factor * inverse
        for w in range(win):
            got = raw[ends.index(w)] * inverse if w in ends else lg[c, part_of(w), :] * factor
            resp[c, part_of(w), :] = got.astype(BF16)
            macc[part_of(w), :] += fold(got)
        cost = xn[c][0:1, :] * (scale2 * LN2) - (top * LN2 + jnp.log(whole))
        for i in range(lanes):
            res_cost[pl.ds(c * lanes + i, 1), :] = cost[:, i * 128 : (i + 1) * 128]
        return carry

    lax.fori_loop(0, nchunk, second, 0)

    def gather(w):
        sums = dot(resp[0, part_of(w), :], chunk_rows(0), NN)
        for c in range(1, nchunk):
            sums = sums + dot(resp[c, part_of(w), :], chunk_rows(c), NN)
        acc[part_of(w), :] = sums

    on(moved, each(lambda: [traded(res_cost, cost_ref, 3, f_send, f_recv)], lambda one: one.start()))
    for d, w in ((0, 0), (1, win - 1)):
        gather(w)
        ship(d, 2, w)
    for w in range(1, win - 1):
        gather(w)
    def give(n):
        low, high = ((cb, (blk - 1) * cb), (0, cb), ((blk - 1) * cb, blk * cb))[n]
        part = pl.ds(low, high - low)

        def here():
            out_ref[part, :] = res[part, :]

        on(stays, here)
        on(moved, each(lambda: [given(n)], lambda one: one.start()))

    def given(n):
        if n == 3:
            return traded(res_cost, cost_ref, 3, f_send, f_recv)
        low, high = ((cb, (blk - 1) * cb), (0, cb), ((blk - 1) * cb, blk * cb))[n]
        part = pl.ds(low, high - low)
        return traded(res.at[part], out_ref.at[part], n, f_send, f_recv)

    for w in range(2, win - 2):
        res[part_of(w - 1), :] = fresh(w)
    give(0)
    for n, d, w in ((1, 1, 1), (2, 0, win - 2)):
        land(d, 2)
        res[part_of(w - 1), :] = fresh(w, (d, 2))
        give(n)

    def cost_here():
        cost_ref[...] = res_cost[...]

    on(stays, cost_here)

    for d in range(2):
        @pl.when(holds[d])
        def _():
            block_copy(d).wait_send()

        @pl.when(sides[d])
        def _():
            for q in range(3):
                for copy in edge_copies(d, q):
                    copy.wait_send()

    on(moved, each(trades, lambda one: one.wait_send()))
    on(moved, each(lambda: [given(n) for n in range(4)], lambda one: one.wait()))

    if fused:
        def drain(k, carry):
            row_copy(me, lax.rem(wid + k, total_n)).wait_send()
            return carry

        lax.fori_loop(1, total_n, drain, 0)


def regroup(sample_rows, destination, own_n, rep_n):
    count, feat = sample_rows.shape
    pp = count // (own_n * rep_n)
    target = destination // count
    outgoing = jnp.zeros((own_n, rep_n, pp, feat), sample_rows.dtype)
    outgoing = outgoing.at[target // rep_n, target % rep_n, destination % pp].set(sample_rows)
    arrived = lax.all_to_all(
        lax.all_to_all(outgoing, "own", split_axis=0, concat_axis=0, tiled=True),
        "rep", split_axis=1, concat_axis=1, tiled=True,
    )
    return arrived.reshape(count, feat)


def per_device(sample_rows, destination, neighbours, centroids):
    own_n = lax.axis_size("own")
    rep_n = lax.axis_size("rep")
    count, feat = sample_rows.shape
    blk, _, cb, _ = centroids.shape
    pp = count // (own_n * rep_n)
    chunk = min(256, count)
    nchunk = count // chunk
    fused = pp % 16 == 0 and pp & (pp - 1) == 0 and chunk % pp == 0
    rows = sample_rows if fused else regroup(sample_rows, destination, own_n, rep_n)
    order = [j for j in (2, 1, 3) if j < nchunk] + list(range(4, nchunk)) + [0]
    wc = (blk + 2) * cb
    total_n = own_n * rep_n
    dma = pltpu.SemaphoreType.DMA
    vmem = pl.BlockSpec(memory_space=pltpu.VMEM)
    staged = count if fused else 16
    out, cost = pl.pallas_call(
        functools.partial(kernel, fused, own_n, rep_n, pp, chunk, order),
        out_shape=(
            jax.ShapeDtypeStruct((blk * cb, feat), BF16),
            jax.ShapeDtypeStruct((count // 128, 128), F32),
        ),
        in_specs=[pl.BlockSpec(memory_space=pltpu.HBM)] * 4,
        out_specs=(vmem, vmem),
        scratch_shapes=[
            pltpu.VMEM((neighbours.shape[1], count), jnp.int32),
            pltpu.VMEM((1, count), jnp.int32),
            pltpu.VMEM((staged, feat), BF16),
            pltpu.VMEM((count, feat), BF16),
            pltpu.VMEM((staged, feat), BF16),
            pltpu.VMEM((nchunk, 8, chunk), F32),
            pltpu.VMEM((wc, feat), BF16),
            pltpu.VMEM((wc, 1), F32),
            pltpu.VMEM((nchunk, 8, chunk), F32),
            pltpu.VMEM((nchunk, 8, chunk), F32),
            pltpu.VMEM((wc, feat), F32),
            pltpu.VMEM((wc, 128), F32),
            pltpu.VMEM((nchunk, wc, chunk), F32),
            pltpu.VMEM((nchunk, wc, chunk), BF16),
            pltpu.VMEM((2, 3, cb, feat), BF16),
            pltpu.VMEM((2, 3, cb, feat), BF16),
            pltpu.VMEM((2, 3, 8, 128), F32),
            pltpu.VMEM((2, 3, 8, 128), F32),
            dma((total_n,)),
            dma((total_n,)),
            dma((2,)),
            dma((2,)),
            dma((2, 3)),
            dma((2, 3)),
            dma((2, 3)),
            dma((2, 3)),
            dma((4,)),
            dma((2,)),
            dma((2,)),
            dma((4,)),
            dma((4,)),
            pltpu.VMEM((blk * cb, feat), BF16),
            pltpu.VMEM((count // 128, 128), F32),
        ],
        compiler_params=pltpu.CompilerParams(
            collective_id=0, has_side_effects=True, vmem_limit_bytes=64 * 1024 * 1024
        ),
    )(neighbours.T, destination.reshape(1, count), rows, centroids.reshape(blk * cb, feat))
    return out.reshape(centroids.shape), cost.reshape(count)


def solution(mesh):
    return jax.shard_map(
        per_device,
        mesh=mesh,
        in_specs=(
            P(("own", "rep"), None),
            P(("own", "rep")),
            P(("own", "rep"), None),
            P("own", "rep", None, None),
        ),
        out_specs=(P("own", "rep", None, None), P(("own", "rep"))),
        check_vma=False,
    )
```

```python
import functools
import math

import jax
import jax.numpy as jnp
from jax import lax
from jax.experimental import pallas as pl
from jax.experimental.pallas import tpu as pltpu
from jax.sharding import PartitionSpec as P

ITERS = 2
PRIOR = 1.0
MESH = pl.DeviceIdType.MESH
F32 = jnp.float32
BF16 = jnp.bfloat16
LN2 = math.log(2.0)
NT = (((1,), (1,)), ((), ()))
NN = (((1,), (0,)), ((), ()))


def dot(a, b, dims):
    return lax.dot_general(a, b, dims, preferred_element_type=F32)


def kernel(
    fused, own_n, rep_n, pp, chunk, order, *refs
):
    (nbr_in, dest_in, rows_in, cent_in, out_ref, cost_ref,
     nbr_ref, dest_ref, rows_ref, arr, outb, stat, cand, cn, bias, xn, acc, macc, lg, resp, snd, rcv, msnd, mrcv,
     a_send, a_recv, c_send, c_recv, s_send, s_recv, m_send, m_recv, load,
     t_send, t_recv, f_send, f_recv, res, res_cost) = refs
    count, feat = rows_in.shape
    slots = nbr_ref.shape[0]
    cb = rcv.shape[2]
    blk = cent_in.shape[0] // cb
    win = blk + 2
    wc = win * cb
    nchunk = count // chunk
    lanes = chunk // 128
    total_n = own_n * rep_n
    own = lax.axis_index("own")
    rep = lax.axis_index("rep")
    me = own * rep_n + rep
    paired = fused and rep_n == 2 and own_n % 2 == 0

    def place_of(a, b):
        if not paired:
            return (a, b)
        odd = lax.rem(a, 2)
        return (a - odd + b, odd)

    work, col = place_of(own, rep)
    wid = work * rep_n + col
    moved = jnp.logical_and(paired, wid != me)
    stays = jnp.logical_not(moved)
    holds = (own > 0, own < own_n - 1)
    sides = (work > 0, work < own_n - 1)
    scale2 = 0.5 / math.sqrt(feat) / LN2

    loads = [
        pltpu.make_async_copy(a, b, load.at[i])
        for i, (a, b) in enumerate((
            (dest_in, dest_ref),
            (rows_in, rows_ref if fused else arr),
            (cent_in, cand.at[pl.ds(cb, blk * cb)]),
            (nbr_in, nbr_ref),
        ))
    ]
    def on(which, fn):
        if paired or which is stays:
            pl.when(which)(fn)

    def traded(src, dst, i, send=t_send, recv=t_recv):
        return pltpu.make_async_remote_copy(
            src_ref=src, dst_ref=dst, send_sem=send.at[i], recv_sem=recv.at[i],
            device_id=(work, col), device_id_type=MESH,
        )

    def trades():
        return [
            traded(nbr_in, nbr_ref, 0),
            traded(cent_in, cand.at[pl.ds(cb, blk * cb)], 1),
        ]

    def each(ops, act):
        def run():
            for one in ops():
                act(one)
        return run

    for one in loads[:2]:
        one.start()
    on(stays, each(lambda: loads[2:], lambda one: one.start()))
    barrier = pltpu.get_barrier_semaphore()
    if fused:
        def greet(k, carry):
            t = lax.rem(me + k, total_n)
            pl.semaphore_signal(
                barrier, inc=1, device_id=(lax.div(t, rep_n), lax.rem(t, rep_n)), device_id_type=MESH
            )
            return carry

        lax.fori_loop(1, total_n, greet, 0)
    else:
        for d in range(2):
            @pl.when(sides[d])
            def _():
                pl.semaphore_signal(
                    barrier, inc=1, device_id=(own + 2 * d - 1, rep), device_id_type=MESH
                )

    zero_block = jnp.zeros((cb, feat), BF16)
    for d in range(2):
        @pl.when(jnp.logical_not(sides[1 - d]))
        def _():
            place = 0 if d else win - 1
            cand[place * cb : (place + 1) * cb, :] = zero_block
            for q in range(3):
                rcv[d, q] = zero_block
                mrcv[d, q] = jnp.zeros((8, 128), F32)

    def block_copy(d):
        src = 0 if d == 0 else (blk - 1) * cb
        dst = (win - 1) * cb if d == 0 else 0
        return pltpu.make_async_remote_copy(
            src_ref=cent_in.at[pl.ds(src, cb)],
            dst_ref=cand.at[pl.ds(dst, cb)],
            send_sem=c_send.at[d],
            recv_sem=c_recv.at[d],
            device_id=place_of(own + 2 * d - 1, rep),
            device_id_type=MESH,
        )

    def edge_copies(d, q):
        where = place_of(work + 2 * d - 1, col)
        return [
            pltpu.make_async_remote_copy(
                src_ref=a.at[d, q], dst_ref=b.at[d, q], send_sem=s.at[d, q], recv_sem=r.at[d, q],
                device_id=where, device_id_type=MESH,
            )
            for a, b, s, r in ((msnd, mrcv, m_send, m_recv), (snd, rcv, s_send, s_recv))
        ]

    def row_copy(src, t):
        return pltpu.make_async_remote_copy(
            src_ref=outb.at[pl.ds(pl.multiple_of(t * pp, pp), pp)],
            dst_ref=arr.at[pl.ds(pl.multiple_of(src * pp, pp), pp)],
            send_sem=a_send.at[t],
            recv_sem=a_recv.at[src],
            device_id=place_of(lax.div(t, rep_n), lax.rem(t, rep_n)),
            device_id_type=MESH,
        )

    per = chunk // pp if fused else 1
    group = lax.div(me, per) if fused else 0

    def pack(g):
        base = pl.multiple_of(g * chunk, chunk)
        pos = lax.broadcasted_iota(jnp.int32, (chunk, count), 0)
        bits = pp.bit_length() - 1
        want = lax.shift_right_logical(pos, bits) * count + (pos & (pp - 1))
        hot = dest_ref[...] - (g * per * count + me * pp)
        pick = jnp.where(want == hot, 1.0, 0.0).astype(BF16)
        outb[pl.ds(base, chunk), :] = dot(pick, rows_ref[...], NN).astype(BF16)

    def wait_entry():
        if fused:
            pl.semaphore_wait(barrier, total_n - 1)
        else:
            for d in range(2):
                @pl.when(sides[d])
                def _():
                    pl.semaphore_wait(barrier, 1)
        on(moved, each(trades, lambda one: one.start()))
        for d in range(2):
            @pl.when(holds[d])
            def _():
                block_copy(d).start()

    def send_group(g):
        def send(k, carry):
            t = g * per + lax.rem(me + k, per)

            @pl.when(t != wid)
            def _():
                row_copy(me, t).start()

            return carry

        lax.fori_loop(0, per, send, 0)

    loads[0].wait()
    loads[1].wait()
    if fused:
        for n, j in enumerate(order):
            g = lax.rem(group + j, nchunk)
            pack(g)
            if n == 0:
                wait_entry()
            send_group(g)
        mine = pl.ds(pl.multiple_of(me * pp, pp), pp)
        kept = pl.ds(pl.multiple_of(wid * pp, pp), pp)
        arr[mine, :] = outb[kept, :]
    else:
        wait_entry()
    rows = arr
    on(stays, each(lambda: loads[2:], lambda one: one.wait()))
    on(moved, each(trades, lambda one: one.wait_recv()))

    for c in range(nchunk):
        ids = nbr_ref[:, c * chunk : (c + 1) * chunk]
        for w in range(win):
            block = (work * blk - 1 + w) * rep_n + col
            hit = ids[0:1] == block
            for m in range(1, slots):
                hit = jnp.logical_or(hit, ids[m : m + 1] == block)
            bias[c, w : w + 1, :] = jnp.where(hit, 0.0, -jnp.inf)

    acc[...] = jnp.zeros_like(acc)
    macc[...] = jnp.zeros_like(macc)

    def part_of(w):
        if isinstance(w, int):
            return pl.ds(w * cb, cb)
        return pl.ds(pl.multiple_of(w * cb, cb), cb)

    def norms(part):
        wide = cand[part, :].astype(F32)
        cn[part, :] = jnp.sum(wide * wide, axis=1, keepdims=True) * scale2

    norms(pl.ds(cb, blk * cb))
    for d in range(2):
        @pl.when(sides[1 - d])
        def _():
            block_copy(d).wait_recv()
    norms(part_of(0))
    norms(part_of(win - 1))

    def fold(got):
        folded = got[:, 0:128]
        for i in range(1, chunk // 128):
            folded = folded + got[:, i * 128 : (i + 1) * 128]
        return folded

    def respond(c):
        raw = [lg[c, w * cb : (w + 1) * cb, :] + bias[c, w : w + 1, :] for w in range(win)]
        top = functools.reduce(jnp.maximum, raw)
        top = jnp.max(top, axis=0, keepdims=True)
        raw = [jnp.exp2(r - top) for r in raw]
        whole = jnp.sum(functools.reduce(jnp.add, raw), axis=0, keepdims=True)
        inverse = 1.0 / whole
        for w in range(win):
            part = slice(w * cb, (w + 1) * cb)
            got = raw[w] * inverse
            resp[c, part, :] = got.astype(BF16)
            macc[part, :] += fold(got)

    def chunk_rows(c):
        return rows[pl.ds(pl.multiple_of(c * chunk, chunk), chunk), :]

    def arrive(c):
        if fused:
            def wait(k, carry):
                s = c * per + k

                @pl.when(s != me)
                def _():
                    row_copy(s, s).wait_recv()

                return carry

            lax.fori_loop(0, per, wait, 0)
        x = chunk_rows(c)
        lg[c] = dot(cand[...], x, NT) * (2.0 * scale2) - cn[...]
        respond(c)
        wide = x.astype(F32)
        wide = wide * wide
        high = wide.astype(BF16)
        low = (wide - high.astype(F32)).astype(BF16)
        ones = jnp.ones((8, feat), BF16)
        xn[c] = dot(ones, high, NT) + dot(ones, low, NT)

    def early(j, carry):
        c = lax.rem(group + j, nchunk)
        arrive(c)
        acc[...] += dot(resp[c], chunk_rows(c), NN)
        return carry

    if nchunk > 1:
        lax.fori_loop(0, nchunk - 1, early, 0)
    last = lax.rem(group + nchunk - 1, nchunk)
    arrive(last)

    def mass_of(w):
        return jnp.sum(macc[part_of(w), :], axis=1, keepdims=True)

    def ship(d, q, w):
        snd[d, q] = acc[part_of(w), :].astype(BF16)
        wide = jnp.transpose(jnp.broadcast_to(mass_of(w), (cb, 128)))
        msnd[d, q] = wide[0:8, :]

        there = work + 2 * d - 1

        @pl.when(jnp.logical_and(there >= 0, there < own_n))
        def _():
            for copy in edge_copies(d, q):
                copy.start()

    def land(d, q):
        there = work + 1 - 2 * d

        @pl.when(jnp.logical_and(there >= 0, there < own_n))
        def _():
            for copy in edge_copies(d, q):
                copy.wait_recv()

    def fresh(w, source=None):
        total = acc[part_of(w), :] + cand[part_of(w), :].astype(F32)
        tally = mass_of(w) + PRIOR
        if source is not None:
            total = total + rcv[source].astype(F32)
            arrived = jnp.transpose(jnp.broadcast_to(mrcv[source][0:1, :], (128, 128)))
            tally = tally + arrived[:, 0:1]
        return (total * (1.0 / tally)).astype(BF16)

    def finish(w):
        acc[part_of(w), :] += dot(resp[last, part_of(w), :], chunk_rows(last), NN)

    def score(w):
        norms(part_of(w))
        for c in range(nchunk):
            lg[c, part_of(w), :] = (
                dot(cand[part_of(w), :], chunk_rows(c), NT) * (2.0 * scale2) - cn[part_of(w), :]
            )

    odd = lax.rem(work, 2)
    even = 1 - odd
    far_out, far_in = odd * (win - 1), 1 + odd * (win - 3)
    near_out, near_in = even * (win - 1), 1 + even * (win - 3)
    for d, q, w in ((odd, 0, far_out), (odd, 1, far_in), (even, 0, near_out), (even, 1, near_in)):
        finish(w)
        ship(d, q, w)
    for w in range(2, win - 2):
        finish(w)
    for w in range(2, win - 2):
        cand[part_of(w), :] = fresh(w)
        score(w)
    def update(d, q, w):
        land(d, q)
        cand[part_of(w), :] = fresh(w, (d, q))
        score(w)

    update(odd, 0, near_in)
    update(odd, 1, near_out)
    update(even, 0, far_in)

    def inner(c, carry):
        raw = [lg[c, part_of(w), :] + bias[c, w : w + 1, :] for w in range(1, win - 1)]
        top = jnp.max(functools.reduce(jnp.maximum, raw), axis=0, keepdims=True)
        raw = [jnp.exp2(r - top) for r in raw]
        for w in range(1, win - 1):
            lg[c, part_of(w), :] = raw[w - 1]
        stat[c, 0:1, :] = top
        stat[c, 1:2, :] = jnp.sum(functools.reduce(jnp.add, raw), axis=0, keepdims=True)
        return carry

    lax.fori_loop(0, nchunk, inner, 0)
    update(even, 1, far_out)
    macc[...] = jnp.zeros_like(macc)

    def second(c, carry):
        ends = (0, win - 1)
        raw = [lg[c, part_of(w), :] + bias[c, w : w + 1, :] for w in ends]
        held = stat[c, 0:1, :]
        top = jnp.maximum(jnp.max(jnp.maximum(*raw), axis=0, keepdims=True), held)
        raw = [jnp.exp2(r - top) for r in raw]
        factor = jnp.exp2(held - top)
        whole = stat[c, 1:2, :] * factor + jnp.sum(raw[0] + raw[1], axis=0, keepdims=True)
        inverse = 1.0 / whole
        factor = factor * inverse
        for w in range(win):
            got = raw[ends.index(w)] * inverse if w in ends else lg[c, part_of(w), :] * factor
            resp[c, part_of(w), :] = got.astype(BF16)
            macc[part_of(w), :] += fold(got)
        cost = xn[c][0:1, :] * (scale2 * LN2) - (top * LN2 + jnp.log(whole))
        for i in range(lanes):
            res_cost[pl.ds(c * lanes + i, 1), :] = cost[:, i * 128 : (i + 1) * 128]
        return carry

    lax.fori_loop(0, nchunk, second, 0)

    def gather(w):
        sums = dot(resp[0, part_of(w), :], chunk_rows(0), NN)
        for c in range(1, nchunk):
            sums = sums + dot(resp[c, part_of(w), :], chunk_rows(c), NN)
        acc[part_of(w), :] = sums

    on(moved, each(lambda: [traded(res_cost, cost_ref, blk, f_send, f_recv)], lambda one: one.start()))
    def given(n, w):
        part = part_of(w - 1)
        return traded(res.at[part], out_ref.at[part], n, f_send, f_recv)

    def give(n, w):
        part = part_of(w - 1)

        def here():
            out_ref[part, :] = res[part, :]

        on(stays, here)
        on(moved, each(lambda: [given(n, w)], lambda one: one.start()))

    gather(far_out)
    ship(odd, 2, far_out)
    for w in range(2, win - 2):
        gather(w)
        res[part_of(w - 1), :] = fresh(w)
        give(w, w)
        if w == 2:
            gather(near_out)
            ship(even, 2, near_out)
    gather(near_in)
    gather(far_in)
    for n, d, w in ((0, odd, near_in), (1, even, far_in)):
        land(d, 2)
        res[part_of(w - 1), :] = fresh(w, (d, 2))
        give(n, w)

    def cost_here():
        cost_ref[...] = res_cost[...]

    on(stays, cost_here)

    for d in range(2):
        @pl.when(holds[d])
        def _():
            block_copy(d).wait_send()

        @pl.when(sides[d])
        def _():
            for q in range(3):
                for copy in edge_copies(d, q):
                    copy.wait_send()

    on(moved, each(trades, lambda one: one.wait_send()))
    def returned():
        for n in range(blk + 1):
            one = given(n, 1) if n < blk else traded(res_cost, cost_ref, blk, f_send, f_recv)
            one.wait()

    on(moved, returned)

    if fused:
        def drain(k, carry):
            row_copy(me, lax.rem(wid + k, total_n)).wait_send()
            return carry

        lax.fori_loop(1, total_n, drain, 0)


def regroup(sample_rows, destination, own_n, rep_n):
    count, feat = sample_rows.shape
    pp = count // (own_n * rep_n)
    target = destination // count
    outgoing = jnp.zeros((own_n, rep_n, pp, feat), sample_rows.dtype)
    outgoing = outgoing.at[target // rep_n, target % rep_n, destination % pp].set(sample_rows)
    arrived = lax.all_to_all(
        lax.all_to_all(outgoing, "own", split_axis=0, concat_axis=0, tiled=True),
        "rep", split_axis=1, concat_axis=1, tiled=True,
    )
    return arrived.reshape(count, feat)


def per_device(sample_rows, destination, neighbours, centroids):
    own_n = lax.axis_size("own")
    rep_n = lax.axis_size("rep")
    count, feat = sample_rows.shape
    blk, _, cb, _ = centroids.shape
    pp = count // (own_n * rep_n)
    chunk = min(256, count)
    nchunk = count // chunk
    fused = pp % 16 == 0 and pp & (pp - 1) == 0 and chunk % pp == 0
    rows = sample_rows if fused else regroup(sample_rows, destination, own_n, rep_n)
    order = [j for j in (2, 1, 3) if j < nchunk] + list(range(4, nchunk)) + [0]
    wc = (blk + 2) * cb
    total_n = own_n * rep_n
    dma = pltpu.SemaphoreType.DMA
    vmem = pl.BlockSpec(memory_space=pltpu.VMEM)
    staged = count if fused else 16
    out, cost = pl.pallas_call(
        functools.partial(kernel, fused, own_n, rep_n, pp, chunk, order),
        out_shape=(
            jax.ShapeDtypeStruct((blk * cb, feat), BF16),
            jax.ShapeDtypeStruct((count // 128, 128), F32),
        ),
        in_specs=[pl.BlockSpec(memory_space=pltpu.HBM)] * 4,
        out_specs=(vmem, vmem),
        scratch_shapes=[
            pltpu.VMEM((neighbours.shape[1], count), jnp.int32),
            pltpu.VMEM((1, count), jnp.int32),
            pltpu.VMEM((staged, feat), BF16),
            pltpu.VMEM((count, feat), BF16),
            pltpu.VMEM((staged, feat), BF16),
            pltpu.VMEM((nchunk, 8, chunk), F32),
            pltpu.VMEM((wc, feat), BF16),
            pltpu.VMEM((wc, 1), F32),
            pltpu.VMEM((nchunk, 8, chunk), F32),
            pltpu.VMEM((nchunk, 8, chunk), F32),
            pltpu.VMEM((wc, feat), F32),
            pltpu.VMEM((wc, 128), F32),
            pltpu.VMEM((nchunk, wc, chunk), F32),
            pltpu.VMEM((nchunk, wc, chunk), BF16),
            pltpu.VMEM((2, 3, cb, feat), BF16),
            pltpu.VMEM((2, 3, cb, feat), BF16),
            pltpu.VMEM((2, 3, 8, 128), F32),
            pltpu.VMEM((2, 3, 8, 128), F32),
            dma((total_n,)),
            dma((total_n,)),
            dma((2,)),
            dma((2,)),
            dma((2, 3)),
            dma((2, 3)),
            dma((2, 3)),
            dma((2, 3)),
            dma((4,)),
            dma((2,)),
            dma((2,)),
            dma((blk + 1,)),
            dma((blk + 1,)),
            pltpu.VMEM((blk * cb, feat), BF16),
            pltpu.VMEM((count // 128, 128), F32),
        ],
        compiler_params=pltpu.CompilerParams(
            collective_id=0, has_side_effects=True, vmem_limit_bytes=64 * 1024 * 1024
        ),
    )(neighbours.T, destination.reshape(1, count), rows, centroids.reshape(blk * cb, feat))
    return out.reshape(centroids.shape), cost.reshape(count)


def solution(mesh):
    return jax.shard_map(
        per_device,
        mesh=mesh,
        in_specs=(
            P(("own", "rep"), None),
            P(("own", "rep")),
            P(("own", "rep"), None),
            P("own", "rep", None, None),
        ),
        out_specs=(P("own", "rep", None, None), P(("own", "rep"))),
        check_vma=False,
    )
```

```python
import functools
import math

import jax
import jax.numpy as jnp
from jax import lax
from jax.experimental import pallas as pl
from jax.experimental.pallas import tpu as pltpu
from jax.sharding import PartitionSpec as P

ITERS = 2
PRIOR = 1.0
MESH = pl.DeviceIdType.MESH
F32 = jnp.float32
BF16 = jnp.bfloat16
LN2 = math.log(2.0)
NT = (((1,), (1,)), ((), ()))
NN = (((1,), (0,)), ((), ()))


def dot(a, b, dims):
    return lax.dot_general(a, b, dims, preferred_element_type=F32)


def kernel(
    fused, own_n, rep_n, pp, chunk, order, *refs
):
    (nbr_in, dest_in, rows_in, cent_in, out_ref, cost_ref,
     nbr_ref, dest_ref, rows_ref, arr, outb, stat, cand, cn, bias, xn, acc, macc, lg, resp, snd, rcv, msnd, mrcv,
     a_send, a_recv, c_send, c_recv, s_send, s_recv, m_send, m_recv, load,
     t_send, t_recv, f_send, f_recv, res, res_cost) = refs
    count, feat = rows_in.shape
    slots = nbr_ref.shape[0]
    cb = rcv.shape[2]
    blk = cent_in.shape[0] // cb
    win = blk + 2
    wc = win * cb
    nchunk = count // chunk
    lanes = chunk // 128
    total_n = own_n * rep_n
    own = lax.axis_index("own")
    rep = lax.axis_index("rep")
    me = own * rep_n + rep
    paired = fused and rep_n == 2 and own_n % 2 == 0

    def place_of(a, b):
        if not paired:
            return (a, b)
        odd = lax.rem(a, 2)
        return (a - odd + b, odd)

    work, col = place_of(own, rep)
    wid = work * rep_n + col
    moved = jnp.logical_and(paired, wid != me)
    stays = jnp.logical_not(moved)
    holds = (own > 0, own < own_n - 1)
    sides = (work > 0, work < own_n - 1)
    scale2 = 0.5 / math.sqrt(feat) / LN2

    loads = [
        pltpu.make_async_copy(a, b, load.at[i])
        for i, (a, b) in enumerate((
            (dest_in, dest_ref),
            (rows_in, rows_ref if fused else arr),
            (cent_in, cand.at[pl.ds(cb, blk * cb)]),
            (nbr_in, nbr_ref),
        ))
    ]
    def on(which, fn):
        if paired or which is stays:
            pl.when(which)(fn)

    def traded(src, dst, i, send=t_send, recv=t_recv):
        return pltpu.make_async_remote_copy(
            src_ref=src, dst_ref=dst, send_sem=send.at[i], recv_sem=recv.at[i],
            device_id=(work, col), device_id_type=MESH,
        )

    def trades():
        return [
            traded(nbr_in, nbr_ref, 0),
            traded(cent_in, cand.at[pl.ds(cb, blk * cb)], 1),
        ]

    def each(ops, act):
        def run():
            for one in ops():
                act(one)
        return run

    for one in loads[:2]:
        one.start()
    on(stays, each(lambda: loads[2:], lambda one: one.start()))
    barrier = pltpu.get_barrier_semaphore()
    if fused:
        def greet(k, carry):
            t = lax.rem(me + k, total_n)
            pl.semaphore_signal(
                barrier, inc=1, device_id=(lax.div(t, rep_n), lax.rem(t, rep_n)), device_id_type=MESH
            )
            return carry

        lax.fori_loop(1, total_n, greet, 0)
    else:
        for d in range(2):
            @pl.when(sides[d])
            def _():
                pl.semaphore_signal(
                    barrier, inc=1, device_id=(own + 2 * d - 1, rep), device_id_type=MESH
                )

    zero_block = jnp.zeros((cb, feat), BF16)
    for d in range(2):
        @pl.when(jnp.logical_not(sides[1 - d]))
        def _():
            place = 0 if d else win - 1
            cand[place * cb : (place + 1) * cb, :] = zero_block
            for q in range(3):
                rcv[d, q] = zero_block
                mrcv[d, q] = jnp.zeros((8, 128), F32)

    def block_copy(d):
        src = 0 if d == 0 else (blk - 1) * cb
        dst = (win - 1) * cb if d == 0 else 0
        return pltpu.make_async_remote_copy(
            src_ref=cent_in.at[pl.ds(src, cb)],
            dst_ref=cand.at[pl.ds(dst, cb)],
            send_sem=c_send.at[d],
            recv_sem=c_recv.at[d],
            device_id=place_of(own + 2 * d - 1, rep),
            device_id_type=MESH,
        )

    def edge_copies(d, q):
        where = place_of(work + 2 * d - 1, col)
        return [
            pltpu.make_async_remote_copy(
                src_ref=a.at[d, q], dst_ref=b.at[d, q], send_sem=s.at[d, q], recv_sem=r.at[d, q],
                device_id=where, device_id_type=MESH,
            )
            for a, b, s, r in ((msnd, mrcv, m_send, m_recv), (snd, rcv, s_send, s_recv))
        ]

    def row_copy(src, t):
        return pltpu.make_async_remote_copy(
            src_ref=outb.at[pl.ds(pl.multiple_of(t * pp, pp), pp)],
            dst_ref=arr.at[pl.ds(pl.multiple_of(src * pp, pp), pp)],
            send_sem=a_send.at[t],
            recv_sem=a_recv.at[src],
            device_id=place_of(lax.div(t, rep_n), lax.rem(t, rep_n)),
            device_id_type=MESH,
        )

    per = chunk // pp if fused else 1
    group = lax.div(me, per) if fused else 0

    def pack(g):
        base = pl.multiple_of(g * chunk, chunk)
        pos = lax.broadcasted_iota(jnp.int32, (chunk, count), 0)
        bits = pp.bit_length() - 1
        want = lax.shift_right_logical(pos, bits) * count + (pos & (pp - 1))
        hot = dest_ref[...] - (g * per * count + me * pp)
        pick = jnp.where(want == hot, 1.0, 0.0).astype(BF16)
        outb[pl.ds(base, chunk), :] = dot(pick, rows_ref[...], NN).astype(BF16)

    def wait_entry():
        if fused:
            pl.semaphore_wait(barrier, total_n - 1)
        else:
            for d in range(2):
                @pl.when(sides[d])
                def _():
                    pl.semaphore_wait(barrier, 1)
        on(moved, each(trades, lambda one: one.start()))
        for d in range(2):
            @pl.when(holds[d])
            def _():
                block_copy(d).start()

    def send_group(g):
        def send(k, carry):
            t = g * per + lax.rem(me + k, per)

            @pl.when(t != wid)
            def _():
                row_copy(me, t).start()

            return carry

        lax.fori_loop(0, per, send, 0)

    loads[0].wait()
    loads[1].wait()
    if fused:
        for n, j in enumerate(order):
            g = lax.rem(group + j, nchunk)
            pack(g)
            if n == 0:
                wait_entry()
            send_group(g)
        mine = pl.ds(pl.multiple_of(me * pp, pp), pp)
        kept = pl.ds(pl.multiple_of(wid * pp, pp), pp)
        arr[mine, :] = outb[kept, :]
    else:
        wait_entry()
    rows = arr
    on(stays, each(lambda: loads[2:], lambda one: one.wait()))
    on(moved, each(trades, lambda one: one.wait_recv()))

    for c in range(nchunk):
        ids = nbr_ref[:, c * chunk : (c + 1) * chunk]
        for w in range(win):
            block = (work * blk - 1 + w) * rep_n + col
            hit = ids[0:1] == block
            for m in range(1, slots):
                hit = jnp.logical_or(hit, ids[m : m + 1] == block)
            bias[c, w : w + 1, :] = jnp.where(hit, 0.0, -jnp.inf)

    acc[...] = jnp.zeros_like(acc)
    macc[...] = jnp.zeros_like(macc)

    def part_of(w):
        if isinstance(w, int):
            return pl.ds(w * cb, cb)
        return pl.ds(pl.multiple_of(w * cb, cb), cb)

    def norms(part):
        wide = cand[part, :].astype(F32)
        cn[part, :] = jnp.sum(wide * wide, axis=1, keepdims=True) * scale2

    norms(pl.ds(cb, blk * cb))
    for d in range(2):
        @pl.when(sides[1 - d])
        def _():
            block_copy(d).wait_recv()
    norms(part_of(0))
    norms(part_of(win - 1))

    def fold(got):
        folded = got[:, 0:128]
        for i in range(1, chunk // 128):
            folded = folded + got[:, i * 128 : (i + 1) * 128]
        return folded

    def respond(c):
        raw = [lg[c, w * cb : (w + 1) * cb, :] + bias[c, w : w + 1, :] for w in range(win)]
        top = functools.reduce(jnp.maximum, raw)
        top = jnp.max(top, axis=0, keepdims=True)
        raw = [jnp.exp2(r - top) for r in raw]
        whole = jnp.sum(functools.reduce(jnp.add, raw), axis=0, keepdims=True)
        inverse = 1.0 / whole
        for w in range(win):
            part = slice(w * cb, (w + 1) * cb)
            got = raw[w] * inverse
            resp[c, part, :] = got.astype(BF16)
            macc[part, :] += fold(got)

    def chunk_rows(c):
        return rows[pl.ds(pl.multiple_of(c * chunk, chunk), chunk), :]

    def arrive(c):
        if fused:
            def wait(k, carry):
                s = c * per + k

                @pl.when(s != me)
                def _():
                    row_copy(s, s).wait_recv()

                return carry

            lax.fori_loop(0, per, wait, 0)
        x = chunk_rows(c)
        lg[c] = dot(cand[...], x, NT) * (2.0 * scale2) - cn[...]
        respond(c)
        wide = x.astype(F32)
        wide = wide * wide
        high = wide.astype(BF16)
        low = (wide - high.astype(F32)).astype(BF16)
        ones = jnp.ones((8, feat), BF16)
        xn[c] = dot(ones, high, NT) + dot(ones, low, NT)

    def taken(j):
        if nchunk != 4:
            return j
        return jnp.where(j == 3, 1, jnp.where(j == 0, 0, j + 1))

    def early(j, carry):
        c = lax.rem(group + taken(j), nchunk)
        arrive(c)
        acc[...] += dot(resp[c], chunk_rows(c), NN)
        return carry

    if nchunk > 1:
        lax.fori_loop(0, nchunk - 1, early, 0)
    last = lax.rem(group + taken(nchunk - 1), nchunk)
    arrive(last)

    def mass_of(w):
        return jnp.sum(macc[part_of(w), :], axis=1, keepdims=True)

    def ship(d, q, w):
        snd[d, q] = acc[part_of(w), :].astype(BF16)
        wide = jnp.transpose(jnp.broadcast_to(mass_of(w), (cb, 128)))
        msnd[d, q] = wide[0:8, :]

        there = work + 2 * d - 1

        @pl.when(jnp.logical_and(there >= 0, there < own_n))
        def _():
            for copy in edge_copies(d, q):
                copy.start()

    def land(d, q):
        there = work + 1 - 2 * d

        @pl.when(jnp.logical_and(there >= 0, there < own_n))
        def _():
            for copy in edge_copies(d, q):
                copy.wait_recv()

    def fresh(w, source=None):
        total = acc[part_of(w), :] + cand[part_of(w), :].astype(F32)
        tally = mass_of(w) + PRIOR
        if source is not None:
            total = total + rcv[source].astype(F32)
            arrived = jnp.transpose(jnp.broadcast_to(mrcv[source][0:1, :], (128, 128)))
            tally = tally + arrived[:, 0:1]
        return (total * (1.0 / tally)).astype(BF16)

    def finish(w):
        acc[part_of(w), :] += dot(resp[last, part_of(w), :], chunk_rows(last), NN)

    def score(w):
        norms(part_of(w))
        for c in range(nchunk):
            lg[c, part_of(w), :] = (
                dot(cand[part_of(w), :], chunk_rows(c), NT) * (2.0 * scale2) - cn[part_of(w), :]
            )

    odd = lax.rem(work, 2)
    even = 1 - odd
    far_out, far_in = odd * (win - 1), 1 + odd * (win - 3)
    near_out, near_in = even * (win - 1), 1 + even * (win - 3)
    for d, q, w in ((odd, 0, far_out), (odd, 1, far_in), (even, 0, near_out), (even, 1, near_in)):
        finish(w)
        ship(d, q, w)
    for w in range(2, win - 2):
        finish(w)
    for w in range(2, win - 2):
        cand[part_of(w), :] = fresh(w)
        score(w)
    def update(d, q, w):
        land(d, q)
        cand[part_of(w), :] = fresh(w, (d, q))
        score(w)

    update(odd, 0, near_in)
    update(odd, 1, near_out)
    update(even, 0, far_in)

    def inner(c, carry):
        raw = [lg[c, part_of(w), :] + bias[c, w : w + 1, :] for w in range(1, win - 1)]
        top = jnp.max(functools.reduce(jnp.maximum, raw), axis=0, keepdims=True)
        raw = [jnp.exp2(r - top) for r in raw]
        for w in range(1, win - 1):
            lg[c, part_of(w), :] = raw[w - 1]
        stat[c, 0:1, :] = top
        stat[c, 1:2, :] = jnp.sum(functools.reduce(jnp.add, raw), axis=0, keepdims=True)
        return carry

    lax.fori_loop(0, nchunk, inner, 0)
    update(even, 1, far_out)
    macc[...] = jnp.zeros_like(macc)

    def second(c, carry):
        ends = (0, win - 1)
        raw = [lg[c, part_of(w), :] + bias[c, w : w + 1, :] for w in ends]
        held = stat[c, 0:1, :]
        top = jnp.maximum(jnp.max(jnp.maximum(*raw), axis=0, keepdims=True), held)
        raw = [jnp.exp2(r - top) for r in raw]
        factor = jnp.exp2(held - top)
        whole = stat[c, 1:2, :] * factor + jnp.sum(raw[0] + raw[1], axis=0, keepdims=True)
        inverse = 1.0 / whole
        factor = factor * inverse
        for w in range(win):
            got = raw[ends.index(w)] * inverse if w in ends else lg[c, part_of(w), :] * factor
            resp[c, part_of(w), :] = got.astype(BF16)
            macc[part_of(w), :] += fold(got)
        cost = xn[c][0:1, :] * (scale2 * LN2) - (top * LN2 + jnp.log(whole))
        for i in range(lanes):
            res_cost[pl.ds(c * lanes + i, 1), :] = cost[:, i * 128 : (i + 1) * 128]
        return carry

    lax.fori_loop(0, nchunk, second, 0)

    def gather(w):
        sums = dot(resp[0, part_of(w), :], chunk_rows(0), NN)
        for c in range(1, nchunk):
            sums = sums + dot(resp[c, part_of(w), :], chunk_rows(c), NN)
        acc[part_of(w), :] = sums

    on(moved, each(lambda: [traded(res_cost, cost_ref, blk, f_send, f_recv)], lambda one: one.start()))
    def given(n, w):
        part = part_of(w - 1)
        return traded(res.at[part], out_ref.at[part], n, f_send, f_recv)

    def give(n, w):
        part = part_of(w - 1)

        def here():
            out_ref[part, :] = res[part, :]

        on(stays, here)
        on(moved, each(lambda: [given(n, w)], lambda one: one.start()))

    gather(far_out)
    ship(odd, 2, far_out)
    for w in range(2, win - 2):
        gather(w)
        res[part_of(w - 1), :] = fresh(w)
        give(w, w)
        if w == 2:
            gather(near_out)
            ship(even, 2, near_out)
    gather(near_in)
    gather(far_in)
    for n, d, w in ((0, odd, near_in), (1, even, far_in)):
        land(d, 2)
        res[part_of(w - 1), :] = fresh(w, (d, 2))
        give(n, w)

    def cost_here():
        cost_ref[...] = res_cost[...]

    on(stays, cost_here)

    for d in range(2):
        @pl.when(holds[d])
        def _():
            block_copy(d).wait_send()

        @pl.when(sides[d])
        def _():
            for q in range(3):
                for copy in edge_copies(d, q):
                    copy.wait_send()

    on(moved, each(trades, lambda one: one.wait_send()))
    def returned():
        for n in range(blk + 1):
            one = given(n, 1) if n < blk else traded(res_cost, cost_ref, blk, f_send, f_recv)
            one.wait()

    on(moved, returned)

    if fused:
        def drain(k, carry):
            row_copy(me, lax.rem(wid + k, total_n)).wait_send()
            return carry

        lax.fori_loop(1, total_n, drain, 0)


def regroup(sample_rows, destination, own_n, rep_n):
    count, feat = sample_rows.shape
    pp = count // (own_n * rep_n)
    target = destination // count
    outgoing = jnp.zeros((own_n, rep_n, pp, feat), sample_rows.dtype)
    outgoing = outgoing.at[target // rep_n, target % rep_n, destination % pp].set(sample_rows)
    arrived = lax.all_to_all(
        lax.all_to_all(outgoing, "own", split_axis=0, concat_axis=0, tiled=True),
        "rep", split_axis=1, concat_axis=1, tiled=True,
    )
    return arrived.reshape(count, feat)


def per_device(sample_rows, destination, neighbours, centroids):
    own_n = lax.axis_size("own")
    rep_n = lax.axis_size("rep")
    count, feat = sample_rows.shape
    blk, _, cb, _ = centroids.shape
    pp = count // (own_n * rep_n)
    chunk = min(256, count)
    nchunk = count // chunk
    fused = pp % 16 == 0 and pp & (pp - 1) == 0 and chunk % pp == 0
    rows = sample_rows if fused else regroup(sample_rows, destination, own_n, rep_n)
    order = [2, 0, 1, 3] if nchunk == 4 else list(range(nchunk))
    wc = (blk + 2) * cb
    total_n = own_n * rep_n
    dma = pltpu.SemaphoreType.DMA
    vmem = pl.BlockSpec(memory_space=pltpu.VMEM)
    staged = count if fused else 16
    out, cost = pl.pallas_call(
        functools.partial(kernel, fused, own_n, rep_n, pp, chunk, order),
        out_shape=(
            jax.ShapeDtypeStruct((blk * cb, feat), BF16),
            jax.ShapeDtypeStruct((count // 128, 128), F32),
        ),
        in_specs=[pl.BlockSpec(memory_space=pltpu.HBM)] * 4,
        out_specs=(vmem, vmem),
        scratch_shapes=[
            pltpu.VMEM((neighbours.shape[1], count), jnp.int32),
            pltpu.VMEM((1, count), jnp.int32),
            pltpu.VMEM((staged, feat), BF16),
            pltpu.VMEM((count, feat), BF16),
            pltpu.VMEM((staged, feat), BF16),
            pltpu.VMEM((nchunk, 8, chunk), F32),
            pltpu.VMEM((wc, feat), BF16),
            pltpu.VMEM((wc, 1), F32),
            pltpu.VMEM((nchunk, 8, chunk), F32),
            pltpu.VMEM((nchunk, 8, chunk), F32),
            pltpu.VMEM((wc, feat), F32),
            pltpu.VMEM((wc, 128), F32),
            pltpu.VMEM((nchunk, wc, chunk), F32),
            pltpu.VMEM((nchunk, wc, chunk), BF16),
            pltpu.VMEM((2, 3, cb, feat), BF16),
            pltpu.VMEM((2, 3, cb, feat), BF16),
            pltpu.VMEM((2, 3, 8, 128), F32),
            pltpu.VMEM((2, 3, 8, 128), F32),
            dma((total_n,)),
            dma((total_n,)),
            dma((2,)),
            dma((2,)),
            dma((2, 3)),
            dma((2, 3)),
            dma((2, 3)),
            dma((2, 3)),
            dma((4,)),
            dma((2,)),
            dma((2,)),
            dma((blk + 1,)),
            dma((blk + 1,)),
            pltpu.VMEM((blk * cb, feat), BF16),
            pltpu.VMEM((count // 128, 128), F32),
        ],
        compiler_params=pltpu.CompilerParams(
            collective_id=0, has_side_effects=True, vmem_limit_bytes=64 * 1024 * 1024
        ),
    )(neighbours.T, destination.reshape(1, count), rows, centroids.reshape(blk * cb, feat))
    return out.reshape(centroids.shape), cost.reshape(count)


def solution(mesh):
    return jax.shard_map(
        per_device,
        mesh=mesh,
        in_specs=(
            P(("own", "rep"), None),
            P(("own", "rep")),
            P(("own", "rep"), None),
            P("own", "rep", None, None),
        ),
        out_specs=(P("own", "rep", None, None), P(("own", "rep"))),
        check_vma=False,
    )
```
